32 devices in a mesh: head: 2 (over x), blk: 16 (over z, y, core).
Axes of the slice: x: 2, y: 2, z: 4, core: 2. Of those that a mesh axis runs over, the one named last changes fastest.
Arguments:
- tokens: bfloat16 [16, 256, 768], P('blk', 'head'), may hold values from -6 to 6
- doc_starts: int32 [16], replicated, may hold values from 0 to 4095, as said below
- w_qkv: bfloat16 [768, 2304], P(('head', 'blk')), may hold values from -0.3125 to 0.3125
- b_query: bfloat16 [768], P(('head', 'blk')), may hold values from -3 to 3
- b_value: bfloat16 [768], P(('head', 'blk')), may hold values from -3 to 3
- w_out: bfloat16 [768, 768], P(('head', 'blk')), may hold values from -1.5 to 1.5
- b_out: bfloat16 [768], P(('head', 'blk')), may hold values from -2 to 2
- gain_attn: bfloat16 [768], P(('head', 'blk')), may hold values from 0.5 to 1.5
- shift_attn: bfloat16 [768], P(('head', 'blk')), may hold values from -2 to 2
- w_in: bfloat16 [768, 3072], P(('head', 'blk')), may hold values from -0.21875 to 0.21875
- b_in: bfloat16 [3072], P(('head', 'blk')), may hold values from -3 to 3
- w_down: bfloat16 [3072, 768], P(('head', 'blk')), may hold values from -0.109375 to 0.109375
- b_down: bfloat16 [768], P(('head', 'blk')), may hold values from -2 to 2
- gain_ffn: bfloat16 [768], P(('head', 'blk')), may hold values from 0.5 to 1.5
- shift_ffn: bfloat16 [768], P(('head', 'blk')), may hold values from -2 to 2
- cotangent: bfloat16 [16, 256, 768], P('blk', 'head'), may hold values from -6 to 6
Outputs:
- layer_out: bfloat16 [16, 256, 768], P('blk', 'head')
- grad_tokens: float32 [16, 256, 768], P('blk', 'head')
- grad_w_qkv: float32 [768, 2304], P(('head', 'blk'))
- grad_b_query: float32 [768], P(('head', 'blk'))
- grad_b_value: float32 [768], P(('head', 'blk'))
- grad_w_out: float32 [768, 768], P(('head', 'blk'))
- grad_b_out: float32 [768], P(('head', 'blk'))
- grad_gain_attn: float32 [768], P(('head', 'blk'))
- grad_shift_attn: float32 [768], P(('head', 'blk'))
- grad_w_in: float32 [768, 3072], P(('head', 'blk'))
- grad_b_in: float32 [3072], P(('head', 'blk'))
- grad_w_down: float32 [3072, 768], P(('head', 'blk'))
- grad_b_down: float32 [768], P(('head', 'blk'))
- grad_gain_ffn: float32 [768], P(('head', 'blk'))
- grad_shift_ffn: float32 [768], P(('head', 'blk'))
The draws below stay inside these ranges and needn't reach their ends.
Inputs may be any that keep to these rules, and one draw needn't show every extreme that they name: `doc_starts`: strictly increasing and the first is 0; a document runs from its start to the next start (the last to the end of the stream); exactly one document has 2304 tokens and every other has fewer.
All inputs are finite; a program needn't handle non-finite values.
Results may differ from the reference program's by a relative error of at most 0.024.
Values may be sent and summed in bfloat16 or wider, within the bound.
No kernel may reach another device: no remote copies, remote signals or barrier semaphores. Data moves between devices by JAX's collectives and lax.ppermute only.
A program may use at most 512 MiB of HBM per device.

```python
import math
import jax
import jax.numpy as jnp
from jax import lax

D = 768
HEADS = 12
HEAD_DIM = 64
FF = 3072
DOCS = 16
BLOCKS = 16
BLOCK_ROWS = 256
TOKENS = 4096


def draw_doc_starts(key, part):
    left_count = DOCS // 2 - 1
    right_count = DOCS // 2 - 2
    longest = 9 * TOKENS // 16
    long_start = jax.random.randint(jax.random.fold_in(key, 5), (1,), TOKENS // 8 + 1, TOKENS // 4 + 1).astype(jnp.int32)
    long_end = long_start + longest
    left_starts = jnp.sort(jax.random.permutation(jax.random.fold_in(key, 11), TOKENS // 8)[:left_count]).astype(jnp.int32) + 1
    right_starts = jnp.sort(jax.random.permutation(jax.random.fold_in(key, 23), TOKENS // 8 - 1)[:right_count]).astype(jnp.int32) + 1 + long_end
    return jnp.concatenate([jnp.zeros((1,), jnp.int32), left_starts, long_start, long_end, right_starts]).astype(jnp.int32)


def raised(values, key, source, target, blocks, factor):
    def block_of(position):
        return (jnp.arange(values.shape[position]) // (values.shape[position] // blocks)).reshape((-1,) + (1,) * (values.ndim - 1 - position))

    first = jax.random.permutation(key, blocks)[block_of(target)]
    second = (block_of(target) + blocks // 2) % blocks
    return jnp.where((block_of(source) == first) | (block_of(source) == second), factor * values, values)


def block_levels(stream_key, extent, split, smallest, top_value):
    level, own = 1.0, jax.random.fold_in(stream_key, 6)
    for position, shards_of in split:
        steps = jnp.exp(jax.random.uniform(jax.random.fold_in(own, position), (shards_of,), jnp.float32, smallest / len(split), top_value / len(split)))
        level = level * jnp.repeat(steps, extent[position] // shards_of).reshape([-1 if axis == position else 1 for axis in range(len(extent))])
    return level


def noise(stream_key, extent, width, bound, pieces=(), kind=jnp.bfloat16):
    level = block_levels(stream_key, extent, pieces, -0.22, 0.18) if pieces else 1.0
    array = jax.random.normal(stream_key, extent, jnp.float32) * width * level
    return jnp.minimum(jnp.maximum(array, -bound), bound).astype(kind)


def heavy_noise(stream_key, extent, width, reach, cuts, heavy, held_as=jnp.bfloat16):
    drawn = width * jax.random.normal(stream_key, extent, jnp.float32)
    if cuts:
        drawn = drawn * block_levels(stream_key, extent, cuts, -0.22, 0.18)
    return jnp.clip(raised(drawn, jax.random.fold_in(stream_key, 3), *heavy), -reach, reach).astype(held_as)


def setup_inputs(seed: int = 0) -> dict:
    splits = jax.random.split(jax.random.key(seed), 17)
    tokens = heavy_noise(splits[0], (BLOCKS, BLOCK_ROWS, D), 1.0, 6.0, ((0, 16), (1, 2)), (0, 2, 16, 2.0))
    doc_starts = draw_doc_starts(jax.random.fold_in(splits[16], 71), 0)
    w_qkv = noise(splits[2], (D, 3 * D), (D // 2) ** -0.5, 0.3125, ((0, 32),))
    b_query = noise(splits[3], (D,), 0.5, 3.0, ((0, 32),))
    b_value = noise(splits[4], (D,), 0.5, 3.0, ((0, 32),))
    w_out = noise(splits[5], (D, D), 16 ** -0.5, 1.5, ((0, 32),))
    b_out = noise(splits[6], (D,), 0.3, 2.0, ((0, 32),))
    gain_attn = jnp.clip(1.0 + 0.1 * jax.random.normal(splits[7], (D,), jnp.float32), 0.5, 1.5).astype(jnp.bfloat16)
    shift_attn = noise(splits[8], (D,), 0.3, 2.0, ((0, 32),))
    w_in = noise(splits[9], (D, FF), D ** -0.5, 0.21875, ((0, 32),))
    b_in = noise(splits[10], (FF,), 0.5, 3.0, ((0, 32),))
    w_down = noise(splits[11], (FF, D), FF ** -0.5, 0.109375, ((0, 32),))
    b_down = noise(splits[12], (D,), 0.3, 2.0, ((0, 32),))
    gain_ffn = jnp.clip(1.0 + 0.1 * jax.random.normal(splits[13], (D,), jnp.float32), 0.5, 1.5).astype(jnp.bfloat16)
    shift_ffn = noise(splits[14], (D,), 0.3, 2.0, ((0, 32),))
    cotangent = noise(splits[15], (BLOCKS, BLOCK_ROWS, D), 1.0, 6.0, ((0, 16), (1, 2)))
    return dict(tokens=tokens, doc_starts=doc_starts, w_qkv=w_qkv, b_query=b_query, b_value=b_value, w_out=w_out, b_out=b_out, gain_attn=gain_attn, shift_attn=shift_attn, w_in=w_in, b_in=b_in, w_down=w_down, b_down=b_down, gain_ffn=gain_ffn, shift_ffn=shift_ffn, cotangent=cotangent)


masked_score = -1e+30
norm_epsilon = 1e-06

@jax.custom_vjp
def low(v):
    return lax.optimization_barrier(v.astype(jnp.bfloat16)).astype(jnp.float32)

@jax.custom_vjp
def low_back(v):
    return v

def low_keep(v):
    return (low(v), None)

def low_pass(kept, grad):
    return (grad,)

def back_keep(v):
    return (v, None)

def back_low(kept, grad):
    return (low(grad),)
low.defvjp(low_keep, low_pass)
low_back.defvjp(back_keep, back_low)

def doc_ids(positions, doc_starts):
    return lax.optimization_barrier(jnp.sum((positions[:, None] >= doc_starts[None, :]).astype(jnp.int32), axis=1)) - 1

def normalize(values, gain, shift):
    centered = values - lax.optimization_barrier(jnp.mean(values, axis=1, keepdims=True))
    inverse_root = lax.rsqrt(lax.optimization_barrier(jnp.mean(centered * centered, axis=1, keepdims=True)) + norm_epsilon)
    return centered * inverse_root * gain + shift

def encoder_layer(inputs, w_qkv, b_query, b_value, w_out, b_out, gain_attn, shift_attn, w_in, b_in, w_down, b_down, gain_ffn, shift_ffn, token_docs):
    highest = lax.Precision.HIGHEST
    scale_factor = 1.0 / math.sqrt(HEAD_DIM)
    projected = jnp.dot(inputs, w_qkv, precision=highest)
    queries = low_back(low(projected[:, :D] + b_query))
    key_flat = low_back(low(projected[:, D:2 * D]))
    value_flat = low_back(low(projected[:, 2 * D:] + b_value))
    block_width = math.gcd(TOKENS, 512)
    key_three = key_flat.reshape(TOKENS, HEADS, HEAD_DIM)
    value_three = value_flat.reshape(TOKENS, HEADS, HEAD_DIM)
    query_blocks = queries.reshape(TOKENS // block_width, block_width, HEADS, HEAD_DIM)
    doc_blocks = token_docs.reshape(TOKENS // block_width, block_width)

    def attend(block_parts):
        query_block, block_docs = block_parts
        scores = low_back(jnp.einsum('qhd,khd->hqk', query_block, key_three, precision=highest) * scale_factor)
        allowed = block_docs[:, None] == token_docs[None, :]
        probability = low(jax.nn.softmax(jnp.where(allowed[None], scores, masked_score), axis=2))
        return jnp.einsum('hqk,khd->qhd', probability, value_three, precision=highest)
    attended = lax.map(jax.checkpoint(attend), (query_blocks, doc_blocks)).reshape(TOKENS, D)
    attended = low_back(low(attended))
    resid_one = low_back(jnp.dot(attended, w_out, precision=highest)) + b_out + inputs
    hidden_one = normalize(resid_one, gain_attn, shift_attn)
    pre_act = low_back(jnp.dot(low(hidden_one), w_in, precision=highest) + b_in)
    activated = low(jax.nn.gelu(pre_act, approximate=True))
    resid_two = low_back(jnp.dot(activated, w_down, precision=highest)) + b_down + hidden_one
    return normalize(resid_two, gain_ffn, shift_ffn)

def reference(tokens, doc_starts, w_qkv, b_query, b_value, w_out, b_out, gain_attn, shift_attn, w_in, b_in, w_down, b_down, gain_ffn, shift_ffn, cotangent):
    token_docs = doc_ids(lax.iota(jnp.int32, TOKENS), doc_starts)
    inputs = tokens.reshape(TOKENS, D).astype(jnp.float32)
    params = tuple((weight_arg.astype(jnp.float32) for weight_arg in (w_qkv, b_query, b_value, w_out, b_out, gain_attn, shift_attn, w_in, b_in, w_down, b_down, gain_ffn, shift_ffn)))
    layer_value, pullback = jax.vjp(partial_layer(token_docs), inputs, *params)
    gradients = pullback(cotangent.reshape(TOKENS, D).astype(jnp.float32))
    return (layer_value.astype(jnp.bfloat16).reshape(BLOCKS, BLOCK_ROWS, D), gradients[0].reshape(BLOCKS, BLOCK_ROWS, D), gradients[1], gradients[2], gradients[3], gradients[4], gradients[5], gradients[6], gradients[7], gradients[8], gradients[9], gradients[10], gradients[11], gradients[12], gradients[13])

def partial_layer(token_docs):

    def apply_layer(inputs, w_qkv, b_query, b_value, w_out, b_out, gain_attn, shift_attn, w_in, b_in, w_down, b_down, gain_ffn, shift_ffn):
        return encoder_layer(inputs, w_qkv, b_query, b_value, w_out, b_out, gain_attn, shift_attn, w_in, b_in, w_down, b_down, gain_ffn, shift_ffn, token_docs)
    return apply_layer
```

```python
from functools import partial

import jax
import jax.numpy as jnp
from jax import lax
from jax.experimental import pallas as pl
from jax.experimental.pallas import tpu as pltpu
from jax.sharding import PartitionSpec as P

HEADS = 12
HEAD_DIM = 64
Z, Y, C = 4, 2, 2
GROUP = HEADS // Z
QW = GROUP * HEAD_DIM
KVW = 2 * QW
LANE = 128
WPAD = 768
VEC_AT = 640
masked_score = -1e30
norm_epsilon = 1e-06
BF = jnp.bfloat16
F32 = jnp.float32
AXES = ("head", "blk")


def dot(a, b, ca=1, cb=0):
    return lax.dot_general(a, b, (((ca,), (cb,)), ((), ())), preferred_element_type=F32)


def place_keys(pos_ref, src_refs, kvs, sems, zo):
    x, z, y, c = pos_ref[0], pos_ref[1], pos_ref[2], pos_ref[3]
    copies = []
    for dc in range(2):
        for dxy in range(4):
            for o in range(zo):
                for k in range(Z):
                    xx = lax.rem(x + dxy // 2, 2)
                    yy = lax.rem(y + dxy % 2, 2)
                    cc = lax.rem(c + dc, 2)
                    zz = lax.rem(z + k, Z)
                    at = (((o * Z + zz) * Y + yy) * C + cc) * 2 + xx
                    copies.append(
                        pltpu.make_async_copy(
                            src_refs[dc].at[dxy, o, k], kvs.at[at], sems.at[len(copies)]
                        )
                    )
    for copy in copies:
        copy.start()
    return copies


def head_mask_rows(block, offset):
    lanes = lax.broadcasted_iota(jnp.int32, block.shape, 1) // HEAD_DIM
    parts = []
    for h in range(GROUP):
        parts.append(jnp.where(lanes == offset[h], block, jnp.zeros_like(block)))
    return jnp.concatenate(parts, axis=0)


def widen_q(q):
    return jnp.concatenate([q, jnp.zeros((q.shape[0], HEAD_DIM), q.dtype)], axis=1)


def widen_v(v):
    return jnp.concatenate(
        [
            jnp.zeros((v.shape[0], HEAD_DIM), v.dtype),
            v[:, 2 * HEAD_DIM :],
            v[:, : 2 * HEAD_DIM],
        ],
        axis=1,
    )


V_ROW = (2, 3, 1)


def allowed_keys(rng_ref, i, first, rows):
    kid = first + lax.broadcasted_iota(jnp.int32, (rows, LANE), 0)
    ok = (kid >= rng_ref[i, 0:1, :]) & (kid < rng_ref[i, 1:2, :])
    return jnp.concatenate([ok] * GROUP, axis=1)


def attention_forward(
    zo, tile, pos_ref, lim_ref, q_ref, rng_ref, kva_ref, kvb_ref, o_ref, ob_ref, lse_ref,
    kvs, qm, m_s, l_s, acc, sems,
):
    copies = place_keys(pos_ref, (kva_ref, kvb_ref), kvs, sems, zo)
    for i in range(Z):
        qm[i] = head_mask_rows(widen_q(q_ref[i]), (0, 1, 2))
    m_s[...] = jnp.full(m_s.shape, masked_score, F32)
    l_s[...] = jnp.zeros(l_s.shape, F32)
    acc[...] = jnp.zeros(acc.shape, F32)
    for copy in copies:
        copy.wait()
    chunks = tile // LANE

    def step(i, j, masked):
        kt = kvs[pl.ds(j * chunks, chunks)].reshape(tile, KVW)
        s = dot(kt[:, :256], qm[i], 1, 1)
        if masked:
            ok = allowed_keys(rng_ref, i, j * tile, tile)
            s = jnp.where(ok, s, masked_score)
        m_old = m_s[i]
        m_new = jnp.maximum(m_old, jnp.max(s, axis=0, keepdims=True))
        p = jnp.exp(s - m_new)
        if masked:
            p = jnp.where(ok, p, 0.0)
        f = jnp.exp(m_old - m_new)
        l_s[i] = l_s[i] * f + jnp.sum(p, axis=0, keepdims=True)
        m_s[i] = m_new
        pv = dot(kt[:, 128:], p.astype(BF), 0, 0)
        for h in range(GROUP):
            r = V_ROW[h] * HEAD_DIM
            acc[i, h] = (
                acc[i, h] * f[:, h * LANE : (h + 1) * LANE]
                + pv[r : r + HEAD_DIM, h * LANE : (h + 1) * LANE]
            )

    def body(j, carry):
        lo, hi = j * tile, (j + 1) * tile
        for i in range(Z):
            live = (lim_ref[i, 1] > lo) & (lim_ref[i, 0] < hi)
            inside = (lim_ref[i, 2] <= lo) & (lim_ref[i, 3] >= hi)
            pl.when(live & inside)(partial(step, i, j, False))
            pl.when(live & jnp.logical_not(inside))(partial(step, i, j, True))
        return carry

    lax.fori_loop(0, kvs.shape[0] // chunks, body, 0)
    for i in range(Z):
        l = l_s[i]
        lse_ref[i] = m_s[i] + jnp.log(l)
        parts = []
        for h in range(GROUP):
            parts.append((acc[i, h] / l[:, h * LANE : (h + 1) * LANE]).T)
        o = jnp.concatenate(parts, axis=1)
        o_ref[i] = o
        ob_ref[i] = o.astype(BF)


def attention_backward(
    zo, tile, pos_ref, lim_ref, q_ref, do_ref, o_ref, lse_ref, rng_ref, kva_ref, kvb_ref,
    dq_ref, dkv_ref, kvs, qm, dom, delta_s, dqt, dk_s, dv_s, sems,
):
    copies = place_keys(pos_ref, (kva_ref, kvb_ref), kvs, sems, zo)
    for i in range(Z):
        qm[i] = head_mask_rows(widen_q(q_ref[i]), (0, 1, 2))
        dom[i] = head_mask_rows(widen_v(do_ref[i]), V_ROW)
        prod = (do_ref[i].astype(F32) * o_ref[i]).T
        rows = []
        for h in range(GROUP):
            rows.append(
                jnp.sum(prod[h * HEAD_DIM : (h + 1) * HEAD_DIM], axis=0, keepdims=True)
            )
        delta_s[i] = jnp.concatenate(rows, axis=1)
    dqt[...] = jnp.zeros(dqt.shape, F32)
    for copy in copies:
        copy.wait()
    chunks = tile // LANE

    def step(i, j, masked):
        kt = kvs[pl.ds(j * chunks, chunks)].reshape(tile, KVW)
        s = dot(kt[:, :256], qm[i], 1, 1)
        p = jnp.exp(s - lse_ref[i])
        if masked:
            ok = allowed_keys(rng_ref, i, j * tile, tile)
            p = jnp.where(ok, p, 0.0)
        dp = dot(kt[:, 128:], dom[i], 1, 1)
        ds = (p * (dp - delta_s[i])).astype(BF)
        dv_s[...] += dot(p.astype(BF), dom[i], 1, 0)
        dk_s[...] += dot(ds, qm[i], 1, 0)
        dq = dot(kt[:, :256], ds, 0, 0)
        for h in range(GROUP):
            dqt[i, h] += dq[h * HEAD_DIM : (h + 1) * HEAD_DIM, h * LANE : (h + 1) * LANE]

    def body(j, carry):
        lo, hi = j * tile, (j + 1) * tile
        dk_s[...] = jnp.zeros(dk_s.shape, F32)
        dv_s[...] = jnp.zeros(dv_s.shape, F32)
        for i in range(Z):
            live = (lim_ref[i, 1] > lo) & (lim_ref[i, 0] < hi)
            inside = (lim_ref[i, 2] <= lo) & (lim_ref[i, 3] >= hi)
            pl.when(live & inside)(partial(step, i, j, False))
            pl.when(live & jnp.logical_not(inside))(partial(step, i, j, True))
        dk, dv = dk_s[...], dv_s[...]
        out = jnp.concatenate([dk[:, :128], dk[:, 128:] + dv[:, :128], dv[:, 128:]], axis=1)
        dkv_ref[pl.ds(j * chunks, chunks)] = out.astype(BF).reshape(chunks, LANE, KVW)
        return carry

    lax.fori_loop(0, kvs.shape[0] // chunks, body, 0)
    for i in range(Z):
        parts = []
        for h in range(GROUP):
            parts.append((dqt[i, h] * (HEAD_DIM**-0.5)).T)
        dq_ref[i] = jnp.concatenate(parts, axis=1).astype(BF)


def vmem():
    return pl.BlockSpec(memory_space=pltpu.VMEM)


def smem():
    return pl.BlockSpec(memory_space=pltpu.SMEM)


def hbm():
    return pl.BlockSpec(memory_space=pl.ANY)


def run_forward(pos, lim, q, rng, kva, kvb, zo):
    tile = 512
    nc = 32 * zo
    return pl.pallas_call(
        partial(attention_forward, zo, tile),
        out_shape=(
            jax.ShapeDtypeStruct((Z, LANE, QW), F32),
            jax.ShapeDtypeStruct((Z, LANE, QW), BF),
            jax.ShapeDtypeStruct((Z, 1, GROUP * LANE), F32),
        ),
        in_specs=[smem(), smem(), vmem(), vmem(), hbm(), hbm()],
        out_specs=(vmem(), vmem(), vmem()),
        scratch_shapes=[
            pltpu.VMEM((nc, LANE, KVW), BF),
            pltpu.VMEM((Z, GROUP * LANE, 256), BF),
            pltpu.VMEM((Z, 1, GROUP * LANE), F32),
            pltpu.VMEM((Z, 1, GROUP * LANE), F32),
            pltpu.VMEM((Z, GROUP, HEAD_DIM, LANE), F32),
            pltpu.SemaphoreType.DMA((8 * zo * Z,)),
        ],
        compiler_params=pltpu.CompilerParams(vmem_limit_bytes=(16 + 4 * zo) << 20),
    )(pos, lim, q, rng, kva, kvb)


def run_backward(pos, lim, q, do, o, lse, rng, kva, kvb, zo):
    tile = 512
    nc = 32 * zo
    return pl.pallas_call(
        partial(attention_backward, zo, tile),
        out_shape=(
            jax.ShapeDtypeStruct((Z, LANE, QW), BF),
            jax.ShapeDtypeStruct((nc, LANE, KVW), BF),
        ),
        in_specs=[smem(), smem(), vmem(), vmem(), vmem(), vmem(), vmem(), hbm(), hbm()],
        out_specs=(vmem(), vmem()),
        scratch_shapes=[
            pltpu.VMEM((nc, LANE, KVW), BF),
            pltpu.VMEM((Z, GROUP * LANE, 256), BF),
            pltpu.VMEM((Z, GROUP * LANE, 256), BF),
            pltpu.VMEM((Z, 1, GROUP * LANE), F32),
            pltpu.VMEM((Z, GROUP, HEAD_DIM, LANE), F32),
            pltpu.VMEM((tile, 256), F32),
            pltpu.VMEM((tile, 256), F32),
            pltpu.SemaphoreType.DMA((8 * zo * Z,)),
        ],
        compiler_params=pltpu.CompilerParams(vmem_limit_bytes=(18 + 7 * zo) << 20),
    )(pos, lim, q, do, o, lse, rng, kva, kvb)


def normalize(values):
    centered = values - jnp.mean(values, axis=1, keepdims=True)
    inverse_root = lax.rsqrt(jnp.mean(centered * centered, axis=1, keepdims=True) + norm_epsilon)
    return (centered * inverse_root, inverse_root)


def normalize_back(grad_norm, normed, inverse_root):
    return inverse_root * (
        grad_norm
        - jnp.mean(grad_norm, axis=1, keepdims=True)
        - normed * jnp.mean(grad_norm * normed, axis=1, keepdims=True)
    )


class Place:
    def __init__(self, nb):
        self.nb = nb
        self.zo = nb // (Z * Y * C)
        self.x = lax.axis_index("head")
        b = lax.axis_index("blk")
        self.c = b % 2
        self.y = b // 2 % 2
        self.z = b // 4 % 4
        self.o = b // 16

    def move(self, a, dx=0, do=0, dz=0, dy=0, dc=0):
        pairs = []
        for x in range(2):
            for o in range(self.zo):
                for z in range(Z):
                    for y in range(Y):
                        for c in range(C):
                            src = (
                                (x + dx) % 2,
                                (o + do) % self.zo,
                                (z + dz) % Z,
                                (y + dy) % Y,
                                (c + dc) % C,
                            )
                            pairs.append((self.lin(*src), self.lin(x, o, z, y, c)))
        return lax.ppermute(a, AXES, pairs)

    def lin(self, x, o, z, y, c):
        return x * self.nb + ((o * Z + z) * Y + y) * C + c

    def trade_z(self, pieces):
        return [pieces[0]] + [self.move(pieces[Z - m], dz=m) for m in range(1, Z)]

    def gather_o(self, a):
        if self.zo == 1:
            return a[None]
        got = jnp.stack([a] + [self.move(a, do=k) for k in range(1, self.zo)])
        return jnp.roll(got, self.o, axis=0)

    def scatter_o(self, a):
        if self.zo == 1:
            return a[0]
        mine = jnp.roll(a, -self.o, axis=0)
        total = mine[0].astype(F32)
        for k in range(1, self.zo):
            total = total + self.move(mine[self.zo - k], do=k).astype(F32)
        return total.astype(a.dtype)


def pick(a, index, axis):
    return lax.dynamic_index_in_dim(a, index, axis, keepdims=False)


def per_device(
    nb,
    tokens,
    doc_starts,
    w_qkv,
    b_query,
    b_value,
    w_out,
    b_out,
    gain_attn,
    shift_attn,
    w_in,
    b_in,
    w_down,
    b_down,
    gain_ffn,
    shift_ffn,
    cotangent,
):
    at = Place(nb)
    zo, x, y, z, c = at.zo, at.x, at.y, at.z, at.c
    inputs = tokens[0]
    rows, D = inputs.shape
    FF = w_in.shape[1]
    S = D // (32)
    R = S // zo
    FS = FF // 32
    FR = FS // zo
    FC = FF // 2
    total_tokens = rows * 2 * nb

    def slab(a):
        g = at.gather_o(a)
        return g.reshape((g.shape[0] * g.shape[1],) + g.shape[2:])

    small = [b_query, b_value, b_out, gain_attn, shift_attn, b_down, gain_ffn, shift_ffn]
    vec_cols = jnp.concatenate(
        [slab(v)[:, None] for v in small] + [slab(b_in).reshape(4, S).T], axis=1
    )
    vec_cols = jnp.pad(vec_cols, ((0, 0), (0, LANE - vec_cols.shape[1])))
    wq = slab(w_qkv).reshape(S, 3, Z, GROUP, HEAD_DIM)
    order = [(1, 0), (1, 1), (1, 2), (2, 2), (2, 0), (2, 1), (0, 0), (0, 1), (0, 2)]
    w4 = jnp.stack([wq[:, a, :, h] for a, h in order], axis=2)
    w4 = w4.transpose(1, 0, 2, 3).reshape(Z, S, 3 * QW)
    w4 = jnp.concatenate(
        [
            w4,
            jnp.zeros((Z, S, VEC_AT - 3 * QW), BF),
            jnp.broadcast_to(vec_cols[None], (Z, S, LANE)),
        ],
        axis=2,
    )
    w4 = jnp.roll(w4, -z, axis=0)
    got = at.trade_z([jnp.concatenate([inputs, w4[m]], axis=0) for m in range(Z)])
    xcol = jnp.concatenate([g[:rows] for g in got], axis=0)
    wz = jnp.roll(jnp.stack([g[rows:] for g in got]), z, axis=0)
    wp = jnp.stack([wz, at.move(wz, dy=1), at.move(wz, dx=1), at.move(wz, dx=1, dy=1)])
    wc = jnp.stack([wp, at.move(wp, dc=1)]).reshape(2, 2, 2, Z, S, WPAD)
    wc = jnp.roll(wc, (c, x, y), axis=(0, 1, 2))
    wfull = wc.reshape(2, 2, 2, Z, zo, R, WPAD).transpose(1, 4, 3, 2, 0, 5, 6).reshape(D, WPAD)
    w_z = wfull[:, : 3 * QW]
    vecs = wfull[:, VEC_AT:].astype(F32).T
    bq = lax.dynamic_slice_in_dim(vecs[0], z * QW, QW, 0)
    bv = lax.dynamic_slice_in_dim(vecs[1], z * QW, QW, 0)
    bias = jnp.concatenate([jnp.zeros((QW,), F32), bv[2 * HEAD_DIM :], bv[: 2 * HEAD_DIM], bq])
    f_bout, f_g1, f_s1, f_bdown, f_g2, f_s2 = [vecs[j] for j in range(2, 8)]
    vslab = wc[..., VEC_AT + 8 : VEC_AT + 12]
    f_bin = pick(vslab, c, 0).transpose(0, 2, 1, 4, 3).reshape(FC).astype(F32)

    projected = (dot(xcol, w_z) + bias[None]).astype(BF)
    kv = projected[:, :KVW].reshape(Z, rows, KVW)
    q = projected[:, KVW:].reshape(Z, rows, QW) * jnp.asarray(HEAD_DIM**-0.5, BF)

    kvo = at.gather_o(kv)
    kva = jnp.stack([kvo, at.move(kvo, dy=1), at.move(kvo, dx=1), at.move(kvo, dx=1, dy=1)])
    kvb = at.move(kva, dc=1)

    zk = (z + jnp.arange(Z)) % Z
    first = ((((at.o * Z + zk) * Y + y) * C + c) * 2 + x) * rows
    tok = first[:, None] + jnp.arange(rows)[None]
    ends = jnp.concatenate([doc_starts[1:], jnp.full((1,), total_tokens, jnp.int32)])
    begun = tok[:, :, None] >= doc_starts[None, None, :]
    start_t = jnp.max(jnp.where(begun, doc_starts[None, None, :], 0), axis=2)
    end_t = jnp.min(jnp.where(ends[None, None, :] > tok[:, :, None], ends[None, None, :], total_tokens), axis=2)
    rng = jnp.stack([start_t, end_t], axis=1)
    lim = jnp.stack([start_t[:, 0], end_t[:, -1], start_t[:, -1], end_t[:, 0]], axis=1)
    pos = jnp.stack([x, z, y, c]).astype(jnp.int32)

    o_att, ob_att, lse = run_forward(pos, lim, q, rng, kva, kvb, zo)

    wi = slab(w_in).reshape(S, 2, zo, Z, Y, C, FR).transpose(5, 0, 1, 3, 4, 2, 6).reshape(2, S, FC)
    wi_other = at.move(pick(wi, 1 - c, 0), dc=1)
    a_piece = jnp.roll(jnp.stack([pick(wi, c, 0), wi_other]), c, axis=0)
    b_piece = jnp.concatenate([slab(w_down), slab(w_out)], axis=0)

    def gather_chips(piece, x_first):
        zp = jnp.stack([piece] + [at.move(piece, dz=k) for k in range(1, Z)])
        zp = jnp.roll(zp, z, axis=0)
        if x_first:
            p1 = jnp.roll(jnp.stack([zp, at.move(zp, dx=1)]), x, axis=0)
            p2 = jnp.roll(jnp.stack([p1, at.move(p1, dy=1)]), y, axis=0)
            return jnp.moveaxis(p2, 0, 2)
        p1 = jnp.roll(jnp.stack([zp, at.move(zp, dy=1)]), y, axis=0)
        p2 = jnp.roll(jnp.stack([p1, at.move(p1, dx=1)]), x, axis=0)
        return jnp.moveaxis(p2, 1, 2)

    wa = gather_chips(a_piece, True)
    wb = gather_chips(b_piece, False)
    win_c = wa.reshape(2, Z, Y, C, zo, R, FC).transpose(0, 4, 1, 2, 3, 5, 6).reshape(D, FC)
    wdn_c = wb[:, :, :, :FS].reshape(FC, D)
    wo = wb[:, :, :, FS:]
    wo = jnp.roll(jnp.stack([wo, at.move(wo, dc=1)]), c, axis=0)
    wo = wo.reshape(C, 2, Z, Y, zo, R, D).transpose(1, 4, 2, 3, 0, 5, 6).reshape(D, D)

    ob = jnp.stack(at.trade_z([ob_att[k] for k in range(Z)]))
    ob = jnp.roll(ob, z, axis=0).transpose(1, 0, 2).reshape(rows, D)
    r1 = dot(ob, wo) + f_bout[None] + inputs.astype(F32)
    n1, rs1 = normalize(r1)
    h1 = n1 * f_g1[None] + f_s1[None]
    h1b = h1.astype(BF)

    def both(a):
        return jnp.roll(jnp.stack([a, at.move(a, dc=1)]), c, axis=0).reshape(2 * rows, -1)

    def split_sum(part):
        p = part.reshape(2, rows, -1)
        return pick(p, c, 0) + at.move(pick(p, 1 - c, 0), dc=1)

    hb = both(h1b)
    u = dot(hb, win_c) + f_bin[None]
    g, gelu_back = jax.vjp(partial(jax.nn.gelu, approximate=True), u)
    gb = g.astype(BF)
    r2 = split_sum(dot(gb, wdn_c)) + f_bdown[None] + h1
    n2, rs2 = normalize(r2)
    layer_out = (n2 * f_g2[None] + f_s2[None]).astype(BF)
    cot = cotangent[0].astype(F32)
    g_gain2 = jnp.sum(cot * n2, axis=0)
    g_shift2 = jnp.sum(cot, axis=0)
    dr2 = normalize_back(cot * f_g2[None], n2, rs2)
    g_bdown = jnp.sum(dr2, axis=0)
    dfb = both(dr2.astype(BF))
    dub = gelu_back(dot(dfb, wdn_c, 1, 1))[0].astype(BF)
    g_bin = jnp.sum(dub.astype(F32), axis=0)
    dh1 = split_sum(dot(dub, win_c, 1, 1)) + dr2
    g_gain1 = jnp.sum(dh1 * n1, axis=0)
    g_shift1 = jnp.sum(dh1, axis=0)
    dr1 = normalize_back(dh1 * f_g1[None], n1, rs1)
    g_bout = jnp.sum(dr1, axis=0)
    dab = dr1.astype(BF)
    dob = dot(dab, wo, 1, 1).astype(BF)
    dobs = jnp.roll(dob.reshape(rows, Z, QW).transpose(1, 0, 2), -z, axis=0)
    do_att = jnp.stack(at.trade_z([dobs[m] for m in range(Z)]))

    dq, dkv = run_backward(pos, lim, q, do_att, o_att, lse, rng, kva, kvb, zo)

    gw_in = dot(hb, dub, 0, 0).astype(BF)
    gw_dn = dot(gb, dfb, 0, 0).astype(BF)
    gw_out = dot(ob, dab, 0, 0)
    ga = gw_in.reshape(2, zo, Z, Y, C, R, FC).transpose(0, 2, 3, 4, 1, 5, 6).reshape(2, Z, Y, C * S, FC)
    go = gw_out.reshape(2, zo, Z, Y, C, R, D).transpose(4, 0, 2, 3, 1, 5, 6).reshape(C, 2, Z, Y, S, D)
    go = (pick(go, c, 0) + at.move(pick(go, 1 - c, 0).astype(BF), dc=1).astype(F32)).astype(BF)
    gb_all = jnp.concatenate([gw_dn.reshape(2, Z, Y, FS, D), go], axis=3)

    def fold(a, axis, index, **kw):
        return (
            pick(a, index, axis).astype(F32)
            + at.move(pick(a, 1 - index, axis), **kw).astype(F32)
        ).astype(BF)

    def sum_z(a):
        a = jnp.roll(a, -z, axis=0)
        return sum(p.astype(F32) for p in at.trade_z([a[m] for m in range(Z)]))

    ga = fold(fold(ga, 0, x, dx=1), 1, y, dy=1)
    ga = sum_z(ga).reshape(C, S, FC)
    gbs = fold(fold(gb_all, 2, y, dy=1), 0, x, dx=1)
    gbs = sum_z(gbs)
    g_wdn = at.scatter_o(gbs[:FS].reshape(zo, FR, D))
    g_wout = at.scatter_o(gbs[FS:].reshape(zo, R, D))
    ga_own = pick(ga, c, 0)
    ga_oth = at.move(pick(ga, 1 - c, 0).astype(BF), dc=1).astype(F32)
    g_win = jnp.roll(jnp.stack([ga_own, ga_oth]), c, axis=0)
    g_win = g_win.reshape(C, S, 2, Z, Y, zo, FR).transpose(1, 2, 5, 3, 4, 0, 6).reshape(S, FF)
    g_win = at.scatter_o(g_win.reshape(zo, R, FF))

    dkv = at.scatter_o(dkv.reshape(zo, Z, Y, C, 2, rows, KVW))
    dkv = fold(dkv, 2, c, dc=1)
    dkv = jnp.roll(dkv, (-y, -x), axis=(1, 2))
    dkv = (
        dkv[:, 0, 0].astype(F32)
        + at.move(dkv[:, 1, 0], dy=1).astype(F32)
        + at.move(dkv[:, 0, 1], dx=1).astype(F32)
        + at.move(dkv[:, 1, 1], dx=1, dy=1).astype(F32)
    )
    dkv = jnp.roll(dkv, -z, axis=0).astype(BF).reshape(Z * rows, KVW)
    dqkv = jnp.concatenate([dkv, dq.reshape(Z * rows, QW)], axis=1)

    dxp = dot(dqkv, w_z, 1, 1).reshape(Z, rows, D)
    dxs = at.trade_z([dxp[0]] + [dxp[m].astype(BF) for m in range(1, Z)])
    grad_inputs = dr1 + sum(p.astype(F32) for p in dxs)

    gw = dot(xcol, dqkv, 0, 0)
    colsum = jnp.sum(dqkv.astype(F32), axis=0)
    g_bq = lax.dynamic_update_slice(jnp.zeros((D,), F32), colsum[KVW:], (z * QW,))
    sv = colsum[QW:KVW]
    sv = jnp.concatenate([sv[HEAD_DIM:], sv[:HEAD_DIM]])
    g_bv = lax.dynamic_update_slice(jnp.zeros((D,), F32), sv, (z * QW,))
    vrows = jnp.stack([g_bq, g_bv, g_bout, g_gain1, g_shift1, g_bdown, g_gain2, g_shift2])

    def by_slab(a):
        a = a.reshape(2, zo, Z, Y, C, R, -1).transpose(4, 0, 3, 2, 1, 5, 6)
        return a.reshape(C, 2, Y, Z, S, -1)

    gbin = g_bin.reshape(2, Z, Y, 4, S).transpose(0, 2, 1, 4, 3)
    gbin = jnp.stack([gbin, jnp.zeros_like(gbin)])
    gbin = jnp.roll(gbin, c, axis=0)
    gq = jnp.concatenate(
        [
            by_slab(gw),
            jnp.zeros((C, 2, Y, Z, S, VEC_AT - 3 * QW), F32),
            by_slab(vrows.T),
            gbin,
            jnp.zeros((C, 2, Y, Z, S, LANE - 12), F32),
        ],
        axis=5,
    ).astype(BF)
    gq = fold(gq, 0, c, dc=1)
    gq = jnp.roll(gq, (-x, -y), axis=(0, 1))
    gq = (
        gq[0, 0].astype(F32)
        + at.move(gq[0, 1], dy=1).astype(F32)
        + at.move(gq[1, 0], dx=1).astype(F32)
        + at.move(gq[1, 1], dx=1, dy=1).astype(F32)
    ).astype(BF)
    gq = jnp.roll(gq, -z, axis=0)
    gq = jnp.roll(jnp.stack(at.trade_z([gq[m] for m in range(Z)])), z, axis=0).astype(F32)
    gwq = gq[:, :, : 3 * QW].reshape(Z, S, 9, HEAD_DIM)
    inv = [order.index((a, h)) for a in range(3) for h in range(GROUP)]
    gwq = jnp.stack([gwq[:, :, i] for i in inv], axis=2).reshape(Z, S, 3, QW)
    gwq = gwq.transpose(1, 2, 0, 3).reshape(S, 3 * D)
    g_wqkv = at.scatter_o(gwq.reshape(zo, R, 3 * D))
    gv = jnp.sum(gq[:, :, VEC_AT:], axis=0)
    outs = [at.scatter_o(gv[:, j].reshape(zo, R)) for j in range(8)]
    g_b_in = at.scatter_o(gv[:, 8:12].T.reshape(zo, FR))
    return (
        layer_out[None],
        grad_inputs[None],
        g_wqkv,
        outs[0],
        outs[1],
        g_wout,
        outs[2],
        outs[3],
        outs[4],
        g_win,
        g_b_in,
        g_wdn,
        outs[5],
        outs[6],
        outs[7],
    )


def solution(mesh):
    nb = mesh.shape["blk"]
    w2 = P(("head", "blk"), None)
    w1 = P(("head", "blk"))
    tok = P("blk", "head", None)
    return jax.shard_map(
        partial(per_device, nb),
        mesh=mesh,
        in_specs=(tok, P(), w2, w1, w1, w2, w1, w1, w1, w2, w1, w2, w1, w1, w1, tok),
        out_specs=(tok, tok, w2, w1, w1, w2, w1, w1, w1, w2, w1, w2, w1, w1, w1),
        check_vma=False,
    )
```

```python
from functools import partial

import jax
import jax.numpy as jnp
from jax import lax
from jax.experimental import pallas as pl
from jax.experimental.pallas import tpu as pltpu
from jax.sharding import PartitionSpec as P

HEADS = 12
HEAD_DIM = 64
Z, Y, C = 4, 2, 2
GROUP = HEADS // Z
QW = GROUP * HEAD_DIM
KVW = 2 * QW
LANE = 128
WPAD = 768
VEC_AT = 640
masked_score = -1e30
norm_epsilon = 1e-06
BF = jnp.bfloat16
F32 = jnp.float32
AXES = ("head", "blk")


def dot(a, b, ca=1, cb=0):
    return lax.dot_general(a, b, (((ca,), (cb,)), ((), ())), preferred_element_type=F32)


PAIRS = ((1, 2), (0, 3))


def key_tile(pos_ref, refs, t):
    x, z, y, c = pos_ref[0], pos_ref[1], pos_ref[2], pos_ref[3]
    o, zz, yy = t // (Z * Y), lax.rem(t // Y, Z), lax.rem(t, Y)
    k, dy = lax.rem(zz - z + Z, Z), lax.rem(yy - y + Y, Y)
    places, first = [], []
    for dc in range(2):
        for dx in range(2):
            places.append((refs[dc], (dx * 2 + dy, o, k)))
            first.append(t * 4 * LANE + lax.rem(c + dc, 2) * 2 * LANE + lax.rem(x + dx, 2) * LANE)
    return places, first


def visit(pos_ref, lim_ref, t, step):
    lo, hi = t * 4 * LANE, (t + 1) * 4 * LANE
    for pair in PAIRS:
        ks = [lax.rem(zz - pos_ref[1] + Z, Z) for zz in pair]
        live = [(lim_ref[k, 1] > lo) & (lim_ref[k, 0] < hi) for k in ks]
        inside = [(lim_ref[k, 2] <= lo) & (lim_ref[k, 3] >= hi) for k in ks]
        both = live[0] & live[1]
        clear = inside[0] & inside[1]
        pl.when(both & clear)(partial(step, t, ks, False))
        pl.when(both & jnp.logical_not(clear))(partial(step, t, ks, True))
        for n in range(2):
            pl.when(live[n] & jnp.logical_not(both))(partial(step, t, ks[n : n + 1], True))


def lanes(parts):
    return parts[0] if len(parts) == 1 else jnp.concatenate(parts, axis=1)


def rows_of(parts):
    return parts[0] if len(parts) == 1 else jnp.concatenate(parts, axis=0)


def head_mask_rows(block, offset):
    lanes = lax.broadcasted_iota(jnp.int32, block.shape, 1) // HEAD_DIM
    parts = []
    for h in range(GROUP):
        parts.append(jnp.where(lanes == offset[h], block, jnp.zeros_like(block)))
    return jnp.concatenate(parts, axis=0)


def widen_q(q):
    return jnp.concatenate([q, jnp.zeros((q.shape[0], HEAD_DIM), q.dtype)], axis=1)


def widen_v(v):
    return jnp.concatenate(
        [
            jnp.zeros((v.shape[0], HEAD_DIM), v.dtype),
            v[:, 2 * HEAD_DIM :],
            v[:, : 2 * HEAD_DIM],
        ],
        axis=1,
    )


V_ROW = (2, 3, 1)


def allowed_keys(rng_ref, ks, first):
    iota = lax.broadcasted_iota(jnp.int32, (LANE, LANE), 0)
    out = []
    for k in ks:
        begin, end = rng_ref[k, 0:1, :], rng_ref[k, 1:2, :]
        ok = rows_of([(iota >= begin - f) & (iota < end - f) for f in first])
        out += [ok] * GROUP
    return lanes(out)


def attention_forward(
    zo, pos_ref, lim_ref, q_ref, rng_ref, kva_ref, kvb_ref, o_ref, ob_ref, lse_ref,
    qm, m_s, l_s, acc,
):
    for i in range(Z):
        qm[i] = head_mask_rows(widen_q(q_ref[i]), (0, 1, 2))
    m_s[...] = jnp.full(m_s.shape, masked_score, F32)
    l_s[...] = jnp.zeros(l_s.shape, F32)
    acc[...] = jnp.zeros(acc.shape, F32)

    def step(t, ks, masked):
        places, first = key_tile(pos_ref, (kva_ref, kvb_ref), t)
        kt = jnp.concatenate([ref[at] for ref, at in places], axis=0)
        s = dot(kt[:, :256], rows_of([qm[k] for k in ks]), 1, 1)
        if masked:
            ok = allowed_keys(rng_ref, ks, first)
            s = jnp.where(ok, s, masked_score)
        m_old = lanes([m_s[k] for k in ks])
        m_new = jnp.maximum(m_old, jnp.max(s, axis=0, keepdims=True))
        p = jnp.exp(s - m_new)
        if masked:
            p = jnp.where(ok, p, 0.0)
        f = jnp.exp(m_old - m_new)
        l_new = lanes([l_s[k] for k in ks]) * f + jnp.sum(p, axis=0, keepdims=True)
        pv = dot(kt[:, 128:], p.astype(BF), 0, 0)
        for n, k in enumerate(ks):
            at = n * GROUP * LANE
            m_s[k] = m_new[:, at : at + GROUP * LANE]
            l_s[k] = l_new[:, at : at + GROUP * LANE]
            for h in range(GROUP):
                r = V_ROW[h] * HEAD_DIM
                c = at + h * LANE
                acc[k, h] = acc[k, h] * f[:, c : c + LANE] + pv[r : r + HEAD_DIM, c : c + LANE]

    def body(t, carry):
        visit(pos_ref, lim_ref, t, step)
        return carry

    lax.fori_loop(0, zo * Z * Y, body, 0)
    for i in range(Z):
        l = l_s[i]
        lse_ref[i] = m_s[i] + jnp.log(l)
        parts = []
        for h in range(GROUP):
            parts.append((acc[i, h] / l[:, h * LANE : (h + 1) * LANE]).T)
        o = jnp.concatenate(parts, axis=1)
        o_ref[i] = o
        ob_ref[i] = o.astype(BF)


def attention_backward(
    zo, pos_ref, lim_ref, q_ref, do_ref, o_ref, lse_ref, rng_ref, kva_ref, kvb_ref,
    dq_ref, dkva_ref, dkvb_ref, qm, dom, delta_s, dqt, dk_s, dv_s,
):
    for i in range(Z):
        qm[i] = head_mask_rows(widen_q(q_ref[i]), (0, 1, 2))
        dom[i] = head_mask_rows(widen_v(do_ref[i]), V_ROW)
        prod = (do_ref[i].astype(F32) * o_ref[i]).T
        parts = []
        for h in range(GROUP):
            parts.append(
                jnp.sum(prod[h * HEAD_DIM : (h + 1) * HEAD_DIM], axis=0, keepdims=True)
            )
        delta_s[i] = jnp.concatenate(parts, axis=1)
    dqt[...] = jnp.zeros(dqt.shape, F32)

    def step(t, ks, masked):
        places, first = key_tile(pos_ref, (kva_ref, kvb_ref), t)
        kt = jnp.concatenate([ref[at] for ref, at in places], axis=0)
        qs = rows_of([qm[k] for k in ks])
        dos = rows_of([dom[k] for k in ks])
        s = dot(kt[:, :256], qs, 1, 1)
        p = jnp.exp(s - lanes([lse_ref[k] for k in ks]))
        if masked:
            p = jnp.where(allowed_keys(rng_ref, ks, first), p, 0.0)
        dp = dot(kt[:, 128:], dos, 1, 1)
        ds = (p * (dp - lanes([delta_s[k] for k in ks]))).astype(BF)
        dv_s[...] += dot(p.astype(BF), dos, 1, 0)
        dk_s[...] += dot(ds, qs, 1, 0)
        dq = dot(kt[:, :256], ds, 0, 0)
        for n, k in enumerate(ks):
            for h in range(GROUP):
                c = (n * GROUP + h) * LANE
                dqt[k, h] += dq[h * HEAD_DIM : (h + 1) * HEAD_DIM, c : c + LANE]

    def body(t, carry):
        dk_s[...] = jnp.zeros(dk_s.shape, F32)
        dv_s[...] = jnp.zeros(dv_s.shape, F32)
        visit(pos_ref, lim_ref, t, step)
        dk, dv = dk_s[...], dv_s[...]
        out = jnp.concatenate([dk[:, :128], dk[:, 128:] + dv[:, :128], dv[:, 128:]], axis=1)
        out = out.astype(BF)
        places, _ = key_tile(pos_ref, (dkva_ref, dkvb_ref), t)
        for n, (ref, at) in enumerate(places):
            ref[at] = out[n * LANE : (n + 1) * LANE]
        return carry

    lax.fori_loop(0, zo * Z * Y, body, 0)
    for i in range(Z):
        parts = []
        for h in range(GROUP):
            parts.append((dqt[i, h] * (HEAD_DIM**-0.5)).T)
        dq_ref[i] = jnp.concatenate(parts, axis=1).astype(BF)


def vmem():
    return pl.BlockSpec(memory_space=pltpu.VMEM)


def smem():
    return pl.BlockSpec(memory_space=pltpu.SMEM)


def run_forward(pos, lim, q, rng, kva, kvb, zo):
    return pl.pallas_call(
        partial(attention_forward, zo),
        out_shape=(
            jax.ShapeDtypeStruct((Z, LANE, QW), F32),
            jax.ShapeDtypeStruct((Z, LANE, QW), BF),
            jax.ShapeDtypeStruct((Z, 1, GROUP * LANE), F32),
        ),
        in_specs=[smem(), smem(), vmem(), vmem(), vmem(), vmem()],
        out_specs=(vmem(), vmem(), vmem()),
        scratch_shapes=[
            pltpu.VMEM((Z, GROUP * LANE, 256), BF),
            pltpu.VMEM((Z, 1, GROUP * LANE), F32),
            pltpu.VMEM((Z, 1, GROUP * LANE), F32),
            pltpu.VMEM((Z, GROUP, HEAD_DIM, LANE), F32),
        ],
        compiler_params=pltpu.CompilerParams(vmem_limit_bytes=(20 + 4 * zo) << 20),
        cost_estimate=pl.CostEstimate(flops=10**10, bytes_accessed=40 << 20, transcendentals=10**7),
    )(pos, lim, q, rng, kva, kvb)


def run_backward(pos, lim, q, do, o, lse, rng, kva, kvb, zo):
    pieces = jax.ShapeDtypeStruct((4, zo, Z, LANE, KVW), BF)
    return pl.pallas_call(
        partial(attention_backward, zo),
        out_shape=(jax.ShapeDtypeStruct((Z, LANE, QW), BF), pieces, pieces),
        in_specs=[smem(), smem()] + [vmem()] * 7,
        out_specs=(vmem(), vmem(), vmem()),
        scratch_shapes=[
            pltpu.VMEM((Z, GROUP * LANE, 256), BF),
            pltpu.VMEM((Z, GROUP * LANE, 256), BF),
            pltpu.VMEM((Z, 1, GROUP * LANE), F32),
            pltpu.VMEM((Z, GROUP, HEAD_DIM, LANE), F32),
            pltpu.VMEM((4 * LANE, 256), F32),
            pltpu.VMEM((4 * LANE, 256), F32),
        ],
        compiler_params=pltpu.CompilerParams(vmem_limit_bytes=min(24 + 7 * zo, 60) << 20),
        cost_estimate=pl.CostEstimate(flops=6 * 10**10, bytes_accessed=60 << 20, transcendentals=10**7),
    )(pos, lim, q, do, o, lse, rng, kva, kvb)


def hidden_grads_kernel(hb_ref, dub_ref, gb_ref, dfb_ref, out_ref, ga, gd):
    ga[...] = dot(hb_ref[...], dub_ref[...], 0, 0).astype(BF)
    gd[...] = dot(gb_ref[...], dfb_ref[...], 0, 0).astype(BF)
    n = ga.shape[0] // (2 * Z * Y)
    m = gd.shape[0] // (2 * Z * Y)
    width = gd.shape[1]
    for x in range(2):
        for z in range(Z):
            for y in range(Y):
                r = ((x * Z + z) * Y + y) * n
                for h in range(2):
                    out_ref[x * Y + y, z, h * n : (h + 1) * n] = ga[r : r + n, h * width : (h + 1) * width]
                r = ((z * Y + y) * 2 + x) * m
                out_ref[x * Y + y, z, 2 * n :] = gd[r : r + m]


def hidden_grads(hb, dub, gb, dfb):
    rows = (2 * hb.shape[1] + gb.shape[1]) // (2 * Z * Y)
    return pl.pallas_call(
        hidden_grads_kernel,
        out_shape=jax.ShapeDtypeStruct((2 * Y, Z, rows, dfb.shape[1]), BF),
        in_specs=[vmem()] * 4,
        out_specs=vmem(),
        scratch_shapes=[
            pltpu.VMEM((hb.shape[1], dub.shape[1]), BF),
            pltpu.VMEM((gb.shape[1], dfb.shape[1]), BF),
        ],
        compiler_params=pltpu.CompilerParams(vmem_limit_bytes=40 << 20),
        cost_estimate=pl.CostEstimate(flops=2 * 10**9, bytes_accessed=4 << 20, transcendentals=0),
    )(hb, dub, gb, dfb)


def normalize(values):
    centered = values - jnp.mean(values, axis=1, keepdims=True)
    inverse_root = lax.rsqrt(jnp.mean(centered * centered, axis=1, keepdims=True) + norm_epsilon)
    return (centered * inverse_root, inverse_root)


def normalize_back(grad_norm, normed, inverse_root):
    return inverse_root * (
        grad_norm
        - jnp.mean(grad_norm, axis=1, keepdims=True)
        - normed * jnp.mean(grad_norm * normed, axis=1, keepdims=True)
    )


class Place:
    def __init__(self, nb):
        self.nb = nb
        self.zo = nb // (Z * Y * C)
        self.x = lax.axis_index("head")
        b = lax.axis_index("blk")
        self.c = b % 2
        self.y = b // 2 % 2
        self.z = b // 4 % 4
        self.o = b // 16

    def move(self, a, dx=0, do=0, dz=0, dy=0, dc=0):
        pairs = []
        for x in range(2):
            for o in range(self.zo):
                for z in range(Z):
                    for y in range(Y):
                        for c in range(C):
                            src = (
                                (x + dx) % 2,
                                (o + do) % self.zo,
                                (z + dz) % Z,
                                (y + dy) % Y,
                                (c + dc) % C,
                            )
                            pairs.append((self.lin(*src), self.lin(x, o, z, y, c)))
        return lax.ppermute(a, AXES, pairs)

    def lin(self, x, o, z, y, c):
        return x * self.nb + ((o * Z + z) * Y + y) * C + c

    def swap_x_c(self, a):
        pairs = []
        for x in range(2):
            for o in range(self.zo):
                for z in range(Z):
                    for y in range(Y):
                        for c in range(C):
                            pairs.append((self.lin(c, o, z, y, x), self.lin(x, o, z, y, c)))
        return lax.ppermute(a, AXES, pairs)

    def chip_groups(self):
        return [
            [self.lin(x, o, z, y, c) for x in range(2) for z in range(Z) for y in range(Y)]
            for o in range(self.zo)
            for c in range(C)
        ]

    def gather_chips(self, a):
        got = lax.all_gather(a, AXES, axis=0, axis_index_groups=self.chip_groups())
        return got.reshape((2, Z, Y) + a.shape)

    def reduce_chips(self, a):
        groups = [
            [self.lin(x, o, z, y, c) for x in range(2) for y in range(Y)]
            for o in range(self.zo)
            for z in range(Z)
            for c in range(C)
        ]
        return lax.psum_scatter(a, AXES, scatter_dimension=0, axis_index_groups=groups)

    def reduce_z(self, a):
        groups = [
            [self.lin(x, o, z, y, c) for z in range(Z)]
            for x in range(2)
            for o in range(self.zo)
            for y in range(Y)
            for c in range(C)
        ]
        return lax.psum_scatter(a, AXES, scatter_dimension=0, axis_index_groups=groups)

    def trade_z(self, pieces):
        return [pieces[0]] + [self.move(pieces[Z - m], dz=m) for m in range(1, Z)]

    def gather_o(self, a):
        if self.zo == 1:
            return a[None]
        got = jnp.stack([a] + [self.move(a, do=k) for k in range(1, self.zo)])
        return jnp.roll(got, self.o, axis=0)

    def scatter_o(self, a):
        if self.zo == 1:
            return a[0]
        mine = jnp.roll(a, -self.o, axis=0)
        total = mine[0].astype(F32)
        for k in range(1, self.zo):
            total = total + self.move(mine[self.zo - k], do=k).astype(F32)
        return total.astype(a.dtype)


def after(a, dep):
    first = dep[(slice(0, 1),) * dep.ndim].reshape(())
    return a + (first.astype(F32) * 0.0).astype(a.dtype)


def pick(a, index, axis):
    return lax.dynamic_index_in_dim(a, index, axis, keepdims=False)


def per_device(
    nb,
    tokens,
    doc_starts,
    w_qkv,
    b_query,
    b_value,
    w_out,
    b_out,
    gain_attn,
    shift_attn,
    w_in,
    b_in,
    w_down,
    b_down,
    gain_ffn,
    shift_ffn,
    cotangent,
):
    at = Place(nb)
    zo, x, y, z, c = at.zo, at.x, at.y, at.z, at.c
    inputs = tokens[0]
    rows, D = inputs.shape
    FF = w_in.shape[1]
    S = D // (32)
    R = S // zo
    FS = FF // 32
    FR = FS // zo
    FC = FF // 2
    total_tokens = rows * 2 * nb

    def slab(a):
        g = at.gather_o(a)
        return g.reshape((g.shape[0] * g.shape[1],) + g.shape[2:])

    small = [b_query, b_value, b_out, gain_attn, shift_attn, b_down, gain_ffn, shift_ffn]
    vec_cols = jnp.concatenate(
        [slab(v)[:, None] for v in small] + [slab(b_in).reshape(4, S).T], axis=1
    )
    vec_cols = jnp.pad(vec_cols, ((0, 0), (0, LANE - vec_cols.shape[1])))
    wq = slab(w_qkv).reshape(S, 3, Z, GROUP, HEAD_DIM)
    order = [(1, 0), (1, 1), (1, 2), (2, 2), (2, 0), (2, 1), (0, 0), (0, 1), (0, 2)]
    w4 = jnp.stack([wq[:, a, :, h] for a, h in order], axis=2)
    w4 = w4.transpose(1, 0, 2, 3).reshape(Z, S, 3 * QW)
    w4 = jnp.concatenate(
        [
            w4,
            jnp.zeros((Z, S, VEC_AT - 3 * QW), BF),
            jnp.broadcast_to(vec_cols[None], (Z, S, LANE)),
        ],
        axis=2,
    )
    w4 = jnp.roll(w4, -z, axis=0)
    got = at.trade_z([w4[m] for m in range(Z)])
    xcol = jnp.concatenate(at.trade_z([inputs] * Z), axis=0)
    wz = jnp.roll(jnp.stack(got), z, axis=0)
    wp = jnp.stack([wz, at.move(wz, dy=1), at.move(wz, dx=1), at.move(wz, dx=1, dy=1)])
    wp = after(wp, xcol[-8:])
    wc = jnp.stack([wp, at.move(wp, dc=1)]).reshape(2, 2, 2, Z, S, WPAD)
    wc = jnp.roll(wc, (c, x, y), axis=(0, 1, 2))
    wfull = wc.reshape(2, 2, 2, Z, zo, R, WPAD).transpose(1, 4, 3, 2, 0, 5, 6).reshape(D, WPAD)
    w_z = wfull[:, : 3 * QW]
    vecs = wfull[:, VEC_AT:].astype(F32).T
    bq = lax.dynamic_slice_in_dim(vecs[0], z * QW, QW, 0)
    bv = lax.dynamic_slice_in_dim(vecs[1], z * QW, QW, 0)
    bias = jnp.concatenate([jnp.zeros((QW,), F32), bv[2 * HEAD_DIM :], bv[: 2 * HEAD_DIM], bq])
    f_bout, f_g1, f_s1, f_bdown, f_g2, f_s2 = [vecs[j] for j in range(2, 8)]
    vslab = pick(wc[..., VEC_AT + 8 : VEC_AT + 12], c, 1)
    f_bin = vslab.transpose(2, 1, 0, 4, 3).reshape(Z, Y, C, zo, FR)
    f_bin = f_bin.transpose(3, 0, 1, 2, 4).reshape(FC).astype(F32)

    projected = (dot(xcol, w_z) + bias[None]).astype(BF)
    kv = projected[:, :KVW].reshape(Z, rows, KVW)
    q = projected[:, KVW:].reshape(Z, rows, QW) * jnp.asarray(HEAD_DIM**-0.5, BF)

    kvo = at.gather_o(kv)
    kva = jnp.stack([kvo, at.move(kvo, dy=1), at.move(kvo, dx=1), at.move(kvo, dx=1, dy=1)])
    kvb = at.move(kva, dc=1)

    zk = (z + jnp.arange(Z)) % Z
    first = ((((at.o * Z + zk) * Y + y) * C + c) * 2 + x) * rows
    tok = first[:, None] + jnp.arange(rows)[None]
    ends = jnp.concatenate([doc_starts[1:], jnp.full((1,), total_tokens, jnp.int32)])
    begun = tok[:, :, None] >= doc_starts[None, None, :]
    start_t = jnp.max(jnp.where(begun, doc_starts[None, None, :], 0), axis=2)
    end_t = jnp.min(jnp.where(ends[None, None, :] > tok[:, :, None], ends[None, None, :], total_tokens), axis=2)
    rng = jnp.stack([start_t, end_t], axis=1)
    lim = jnp.stack([start_t[:, 0], end_t[:, -1], start_t[:, -1], end_t[:, 0]], axis=1)
    pos = jnp.stack([x, z, y, c]).astype(jnp.int32)

    o_att, ob_att, lse = run_forward(pos, lim, q, rng, kva, kvb, zo)

    wi = slab(w_in).reshape(S, 2, FC)
    wi_other = at.move(pick(wi, 1 - c, 1), dc=1)
    wd = at.swap_x_c(slab(w_down))
    a_piece = jnp.roll(jnp.stack([pick(wi, c, 1), wi_other]), c, axis=0)
    a_piece = a_piece.reshape(2 * S, 2, D).transpose(1, 0, 2).reshape(4 * S, D)
    pack = jnp.concatenate([a_piece, wd, slab(w_out)], axis=0)
    wall = after(at.gather_chips(pack), o_att)

    def natural(a):
        a = a.reshape(2, Z, Y, C, zo, R, -1).transpose(0, 4, 1, 2, 3, 5, 6)
        return a.reshape(D, -1)

    win_c = jnp.concatenate(
        [
            natural(wall[:, :, :, : 2 * S].reshape(2, Z, Y, C, S, D)),
            natural(wall[:, :, :, 2 * S : 4 * S].reshape(2, Z, Y, C, S, D)),
        ],
        axis=1,
    )
    wdn_c = wall[:, :, :, 4 * S : 4 * S + FS].reshape(2, Z, Y, zo, FR, D)
    wdn_c = wdn_c.transpose(3, 1, 2, 0, 4, 5).reshape(FC, D)
    wo = wall[:, :, :, 4 * S + FS :]
    wo = jnp.roll(jnp.stack([wo, at.move(wo, dc=1)]), c, axis=0)
    wo = natural(jnp.moveaxis(wo, 0, 3))

    ob = jnp.stack(at.trade_z([ob_att[k] for k in range(Z)]))
    ob = jnp.roll(ob, z, axis=0).transpose(1, 0, 2).reshape(rows, D)
    r1 = dot(ob, wo) + f_bout[None] + inputs.astype(F32)
    n1, rs1 = normalize(r1)
    h1 = n1 * f_g1[None] + f_s1[None]
    h1b = h1.astype(BF)

    def both(a):
        return jnp.roll(jnp.stack([a, at.move(a, dc=1)]), c, axis=0).reshape(2 * rows, -1)

    def split_sum(part):
        p = part.reshape(2, rows, -1)
        return pick(p, c, 0) + at.move(pick(p, 1 - c, 0), dc=1)

    hb = both(h1b)
    u = dot(hb, win_c) + f_bin[None]
    g, gelu_back = jax.vjp(partial(jax.nn.gelu, approximate=True), u)
    gb = g.astype(BF)
    r2 = split_sum(dot(gb, wdn_c)) + f_bdown[None] + h1
    n2, rs2 = normalize(r2)
    layer_out = (n2 * f_g2[None] + f_s2[None]).astype(BF)
    cot = cotangent[0].astype(F32)
    g_gain2 = jnp.sum(cot * n2, axis=0)
    g_shift2 = jnp.sum(cot, axis=0)
    dr2 = normalize_back(cot * f_g2[None], n2, rs2)
    g_bdown = jnp.sum(dr2, axis=0)
    dfb = both(dr2.astype(BF))
    dub = gelu_back(dot(dfb, wdn_c, 1, 1))[0].astype(BF)
    g_bin = jnp.sum(dub.astype(F32), axis=0)
    hb_s = hb.reshape(2 * rows, 2, zo, Z, Y, C, R).transpose(0, 1, 3, 4, 5, 2, 6).reshape(2 * rows, D)
    gb_s = gb.reshape(2 * rows, zo, Z, Y, 2, FR).transpose(0, 2, 3, 4, 1, 5).reshape(2 * rows, FC)
    by_chip = hidden_grads(hb_s, dub, gb_s, dfb)
    dh1 = split_sum(dot(dub, win_c, 1, 1)) + after(dr2, by_chip)
    g_gain1 = jnp.sum(dh1 * n1, axis=0)
    g_shift1 = jnp.sum(dh1, axis=0)
    dr1 = normalize_back(dh1 * f_g1[None], n1, rs1)
    g_bout = jnp.sum(dr1, axis=0)
    dab = dr1.astype(BF)
    dob = dot(dab, wo, 1, 1).astype(BF)
    dobs = jnp.roll(dob.reshape(rows, Z, QW).transpose(1, 0, 2), -z, axis=0)
    do_att = jnp.stack(at.trade_z([dobs[m] for m in range(Z)]))

    bulk = at.reduce_chips(by_chip)

    def fold(a, axis, index, **kw):
        got = at.move(pick(a, 1 - index, axis), **kw).astype(F32)
        return (pick(a, index, axis).astype(F32) + got).astype(BF)

    dq, dkva, dkvb = run_backward(pos, lim, q, do_att, o_att, lse, rng, kva, kvb, zo)
    dkvb = at.move(dkvb, dc=1)
    dkv = (dkva.astype(F32) + dkvb.astype(F32)).astype(BF)
    dkv = (
        dkv[0].astype(F32)
        + at.move(dkv[1], dy=1).astype(F32)
        + at.move(dkv[2], dx=1).astype(F32)
        + at.move(dkv[3], dx=1, dy=1).astype(F32)
    ).astype(BF)
    dkv = at.scatter_o(dkv).reshape(Z * rows, KVW)
    dqkv = jnp.concatenate([dkv, dq.reshape(Z * rows, QW)], axis=1)

    dxp = dot(dqkv, w_z, 1, 1).reshape(Z, rows, D).astype(BF)
    dx = sum(p.astype(F32) for p in at.trade_z([dxp[m] for m in range(Z)]))
    grad_inputs = dr1 + dx
    bulk = at.reduce_z(bulk).astype(F32)
    ga = jnp.concatenate([bulk[: 2 * S], bulk[2 * S : 4 * S]], axis=1).reshape(C, S, FC)
    g_wdn = at.swap_x_c(bulk[4 * S :].astype(BF)).astype(F32)
    g_wdn = at.scatter_o(g_wdn.reshape(zo, FR, D))
    ga_oth = at.move(pick(ga, 1 - c, 0).astype(BF), dc=1).astype(F32)
    g_win = jnp.roll(jnp.stack([pick(ga, c, 0), ga_oth]), c, axis=0)
    g_win = jnp.concatenate([g_win[0], g_win[1]], axis=1)
    g_win = at.scatter_o(g_win.reshape(zo, R, FF))

    gw = dot(xcol, dqkv, 0, 0)
    colsum = jnp.sum(dqkv.astype(F32), axis=0)
    g_bq = lax.dynamic_update_slice(jnp.zeros((D,), F32), colsum[KVW:], (z * QW,))
    sv = colsum[QW:KVW]
    sv = jnp.concatenate([sv[HEAD_DIM:], sv[:HEAD_DIM]])
    g_bv = lax.dynamic_update_slice(jnp.zeros((D,), F32), sv, (z * QW,))
    vrows = jnp.stack([g_bq, g_bv, g_bout, g_gain1, g_shift1, g_bdown, g_gain2, g_shift2])

    def by_slab(a):
        a = a.reshape(2, zo, Z, Y, C, R, -1).transpose(4, 0, 3, 2, 1, 5, 6)
        return a.reshape(C, 2, Y, Z, S, -1)

    gbin = g_bin.reshape(zo, Z, Y, C, FR).transpose(1, 2, 3, 0, 4).reshape(Z, Y, C, 4, S)
    gbin = gbin.transpose(2, 1, 0, 4, 3)
    gbin = jnp.roll(jnp.stack([gbin, jnp.zeros_like(gbin)], axis=1), c, axis=1)
    gq = jnp.concatenate(
        [
            by_slab(gw),
            jnp.zeros((C, 2, Y, Z, S, VEC_AT - 3 * QW), F32),
            by_slab(vrows.T),
            gbin,
            jnp.zeros((C, 2, Y, Z, S, LANE - 12), F32),
        ],
        axis=5,
    ).astype(BF)
    go = by_slab(dot(ob, dab, 0, 0)).astype(BF)
    gq = jnp.concatenate([gq, go], axis=4)
    gq = fold(gq, 0, c, dc=1)
    gq = jnp.roll(gq, (-x, -y), axis=(0, 1))
    gq = (
        gq[0, 0].astype(F32)
        + at.move(gq[0, 1], dy=1).astype(F32)
        + at.move(gq[1, 0], dx=1).astype(F32)
        + at.move(gq[1, 1], dx=1, dy=1).astype(F32)
    ).astype(BF)
    gq = jnp.roll(gq, -z, axis=0)
    gq = jnp.roll(jnp.stack(at.trade_z([gq[m] for m in range(Z)])), z, axis=0).astype(F32)
    g_wout = at.scatter_o(jnp.sum(gq[:, S:], axis=0).reshape(zo, R, D))
    gq = gq[:, :S]
    gwq = gq[:, :, : 3 * QW].reshape(Z, S, 9, HEAD_DIM)
    inv = [order.index((a, h)) for a in range(3) for h in range(GROUP)]
    gwq = jnp.stack([gwq[:, :, i] for i in inv], axis=2).reshape(Z, S, 3, QW)
    gwq = gwq.transpose(1, 2, 0, 3).reshape(S, 3 * D)
    g_wqkv = at.scatter_o(gwq.reshape(zo, R, 3 * D))
    gv = jnp.sum(gq[:, :, VEC_AT:], axis=0)
    outs = [at.scatter_o(gv[:, j].reshape(zo, R)) for j in range(8)]
    g_b_in = at.scatter_o(gv[:, 8:12].T.reshape(zo, FR))
    return (
        layer_out[None],
        grad_inputs[None],
        g_wqkv,
        outs[0],
        outs[1],
        g_wout,
        outs[2],
        outs[3],
        outs[4],
        g_win,
        g_b_in,
        g_wdn,
        outs[5],
        outs[6],
        outs[7],
    )


def solution(mesh):
    nb = mesh.shape["blk"]
    w2 = P(("head", "blk"), None)
    w1 = P(("head", "blk"))
    tok = P("blk", "head", None)
    return jax.shard_map(
        partial(per_device, nb),
        mesh=mesh,
        in_specs=(tok, P(), w2, w1, w1, w2, w1, w1, w1, w2, w1, w2, w1, w1, w1, tok),
        out_specs=(tok, tok, w2, w1, w1, w2, w1, w1, w1, w2, w1, w2, w1, w1, w1),
        check_vma=False,
    )
```

```python
from functools import partial

import jax
import jax.numpy as jnp
from jax import lax
from jax.experimental import pallas as pl
from jax.experimental.pallas import tpu as pltpu
from jax.sharding import PartitionSpec as P

HEADS = 12
HEAD_DIM = 64
Z, Y, C = 4, 2, 2
GROUP = HEADS // Z
QW = GROUP * HEAD_DIM
KVW = 2 * QW
LANE = 128
WPAD = 768
VEC_AT = 640
masked_score = -1e30
norm_epsilon = 1e-06
BF = jnp.bfloat16
F32 = jnp.float32
AXES = ("head", "blk")


def dot(a, b, ca=1, cb=0):
    return lax.dot_general(a, b, (((ca,), (cb,)), ((), ())), preferred_element_type=F32)


PAIRS = ((1, 2), (0, 3))


def key_tile(pos_ref, refs, t):
    x, z, y, c = pos_ref[0], pos_ref[1], pos_ref[2], pos_ref[3]
    o, zz, yy = t // (Z * Y), lax.rem(t // Y, Z), lax.rem(t, Y)
    k, dy = lax.rem(zz - z + Z, Z), lax.rem(yy - y + Y, Y)
    places, first = [], []
    for dc in range(2):
        for dx in range(2):
            places.append((refs[dc], (dx * 2 + dy, o, k)))
            first.append(t * 4 * LANE + lax.rem(c + dc, 2) * 2 * LANE + lax.rem(x + dx, 2) * LANE)
    return places, first


def visit(pos_ref, lim_ref, t, step):
    lo, hi = t * 4 * LANE, (t + 1) * 4 * LANE
    for pair in PAIRS:
        ks = [lax.rem(zz - pos_ref[1] + Z, Z) for zz in pair]
        live = [(lim_ref[k, 1] > lo) & (lim_ref[k, 0] < hi) for k in ks]
        inside = [(lim_ref[k, 2] <= lo) & (lim_ref[k, 3] >= hi) for k in ks]
        both = live[0] & live[1]
        clear = inside[0] & inside[1]
        pl.when(both & clear)(partial(step, t, ks, False))
        pl.when(both & jnp.logical_not(clear))(partial(step, t, ks, True))
        for n in range(2):
            pl.when(live[n] & jnp.logical_not(both))(partial(step, t, ks[n : n + 1], True))


def lanes(parts):
    return parts[0] if len(parts) == 1 else jnp.concatenate(parts, axis=1)


def rows_of(parts):
    return parts[0] if len(parts) == 1 else jnp.concatenate(parts, axis=0)


def head_mask_rows(block, offset):
    lanes = lax.broadcasted_iota(jnp.int32, block.shape, 1) // HEAD_DIM
    parts = []
    for h in range(GROUP):
        parts.append(jnp.where(lanes == offset[h], block, jnp.zeros_like(block)))
    return jnp.concatenate(parts, axis=0)


def widen_q(q):
    return jnp.concatenate([q, jnp.zeros((q.shape[0], HEAD_DIM), q.dtype)], axis=1)


def widen_v(v):
    return jnp.concatenate(
        [
            jnp.zeros((v.shape[0], HEAD_DIM), v.dtype),
            v[:, 2 * HEAD_DIM :],
            v[:, : 2 * HEAD_DIM],
        ],
        axis=1,
    )


V_ROW = (2, 3, 1)


def allowed_keys(rng_ref, ks, first):
    iota = lax.broadcasted_iota(jnp.int32, (LANE, LANE), 0)
    out = []
    for k in ks:
        begin, end = rng_ref[k, 0:1, :], rng_ref[k, 1:2, :]
        ok = rows_of([(iota >= begin - f) & (iota < end - f) for f in first])
        out += [ok] * GROUP
    return lanes(out)


def attention_forward(
    zo, pos_ref, lim_ref, q_ref, rng_ref, kva_ref, kvb_ref, o_ref, ob_ref, lse_ref,
    qm, m_s, l_s, acc,
):
    for i in range(Z):
        qm[i] = head_mask_rows(widen_q(q_ref[i]), (0, 1, 2))
    m_s[...] = jnp.full(m_s.shape, masked_score, F32)
    l_s[...] = jnp.zeros(l_s.shape, F32)
    acc[...] = jnp.zeros(acc.shape, F32)

    def step(t, ks, masked):
        places, first = key_tile(pos_ref, (kva_ref, kvb_ref), t)
        kt = jnp.concatenate([ref[at] for ref, at in places], axis=0)
        s = dot(kt[:, :256], rows_of([qm[k] for k in ks]), 1, 1)
        if masked:
            ok = allowed_keys(rng_ref, ks, first)
            s = jnp.where(ok, s, masked_score)
        m_old = lanes([m_s[k] for k in ks])
        m_new = jnp.maximum(m_old, jnp.max(s, axis=0, keepdims=True))
        p = jnp.exp(s - m_new)
        if masked:
            p = jnp.where(ok, p, 0.0)
        f = jnp.exp(m_old - m_new)
        l_new = lanes([l_s[k] for k in ks]) * f + jnp.sum(p, axis=0, keepdims=True)
        pv = dot(kt[:, 128:], p.astype(BF), 0, 0)
        for n, k in enumerate(ks):
            at = n * GROUP * LANE
            m_s[k] = m_new[:, at : at + GROUP * LANE]
            l_s[k] = l_new[:, at : at + GROUP * LANE]
            for h in range(GROUP):
                r = V_ROW[h] * HEAD_DIM
                c = at + h * LANE
                acc[k, h] = acc[k, h] * f[:, c : c + LANE] + pv[r : r + HEAD_DIM, c : c + LANE]

    def body(t, carry):
        visit(pos_ref, lim_ref, t, step)
        return carry

    lax.fori_loop(0, zo * Z * Y, body, 0)
    for i in range(Z):
        l = l_s[i]
        lse_ref[i] = m_s[i] + jnp.log(l)
        parts = []
        for h in range(GROUP):
            parts.append((acc[i, h] / l[:, h * LANE : (h + 1) * LANE]).T)
        o = jnp.concatenate(parts, axis=1)
        o_ref[i] = o
        ob_ref[i] = o.astype(BF)


def attention_backward(
    zo, pos_ref, lim_ref, q_ref, do_ref, o_ref, lse_ref, rng_ref, kva_ref, kvb_ref,
    dq_ref, dkva_ref, dkvb_ref, qm, dom, delta_s, dqt, dk_s, dv_s,
):
    for i in range(Z):
        qm[i] = head_mask_rows(widen_q(q_ref[i]), (0, 1, 2))
        dom[i] = head_mask_rows(widen_v(do_ref[i]), V_ROW)
        prod = (do_ref[i].astype(F32) * o_ref[i]).T
        parts = []
        for h in range(GROUP):
            parts.append(
                jnp.sum(prod[h * HEAD_DIM : (h + 1) * HEAD_DIM], axis=0, keepdims=True)
            )
        delta_s[i] = jnp.concatenate(parts, axis=1)
    dqt[...] = jnp.zeros(dqt.shape, F32)

    def step(t, ks, masked):
        places, first = key_tile(pos_ref, (kva_ref, kvb_ref), t)
        kt = jnp.concatenate([ref[at] for ref, at in places], axis=0)
        qs = rows_of([qm[k] for k in ks])
        dos = rows_of([dom[k] for k in ks])
        s = dot(kt[:, :256], qs, 1, 1)
        p = jnp.exp(s - lanes([lse_ref[k] for k in ks]))
        if masked:
            p = jnp.where(allowed_keys(rng_ref, ks, first), p, 0.0)
        dp = dot(kt[:, 128:], dos, 1, 1)
        ds = (p * (dp - lanes([delta_s[k] for k in ks]))).astype(BF)
        dv_s[...] += dot(p.astype(BF), dos, 1, 0)
        dk_s[...] += dot(ds, qs, 1, 0)
        dq = dot(kt[:, :256], ds, 0, 0)
        for n, k in enumerate(ks):
            for h in range(GROUP):
                c = (n * GROUP + h) * LANE
                dqt[k, h] += dq[h * HEAD_DIM : (h + 1) * HEAD_DIM, c : c + LANE]

    def body(t, carry):
        dk_s[...] = jnp.zeros(dk_s.shape, F32)
        dv_s[...] = jnp.zeros(dv_s.shape, F32)
        visit(pos_ref, lim_ref, t, step)
        dk, dv = dk_s[...], dv_s[...]
        out = jnp.concatenate([dk[:, :128], dk[:, 128:] + dv[:, :128], dv[:, 128:]], axis=1)
        out = out.astype(BF)
        places, _ = key_tile(pos_ref, (dkva_ref, dkvb_ref), t)
        for n, (ref, at) in enumerate(places):
            ref[at] = out[n * LANE : (n + 1) * LANE]
        return carry

    lax.fori_loop(0, zo * Z * Y, body, 0)
    for i in range(Z):
        parts = []
        for h in range(GROUP):
            parts.append((dqt[i, h] * (HEAD_DIM**-0.5)).T)
        dq_ref[i] = jnp.concatenate(parts, axis=1).astype(BF)


def vmem():
    return pl.BlockSpec(memory_space=pltpu.VMEM)


def smem():
    return pl.BlockSpec(memory_space=pltpu.SMEM)


def run_forward(pos, lim, q, rng, kva, kvb, zo):
    return pl.pallas_call(
        partial(attention_forward, zo),
        out_shape=(
            jax.ShapeDtypeStruct((Z, LANE, QW), F32),
            jax.ShapeDtypeStruct((Z, LANE, QW), BF),
            jax.ShapeDtypeStruct((Z, 1, GROUP * LANE), F32),
        ),
        in_specs=[smem(), smem(), vmem(), vmem(), vmem(), vmem()],
        out_specs=(vmem(), vmem(), vmem()),
        scratch_shapes=[
            pltpu.VMEM((Z, GROUP * LANE, 256), BF),
            pltpu.VMEM((Z, 1, GROUP * LANE), F32),
            pltpu.VMEM((Z, 1, GROUP * LANE), F32),
            pltpu.VMEM((Z, GROUP, HEAD_DIM, LANE), F32),
        ],
        compiler_params=pltpu.CompilerParams(vmem_limit_bytes=(20 + 4 * zo) << 20),
        cost_estimate=pl.CostEstimate(flops=10**10, bytes_accessed=40 << 20, transcendentals=10**7),
    )(pos, lim, q, rng, kva, kvb)


def run_backward(pos, lim, q, do, o, lse, rng, kva, kvb, zo):
    pieces = jax.ShapeDtypeStruct((4, zo, Z, LANE, KVW), BF)
    return pl.pallas_call(
        partial(attention_backward, zo),
        out_shape=(jax.ShapeDtypeStruct((Z, LANE, QW), BF), pieces, pieces),
        in_specs=[smem(), smem()] + [vmem()] * 7,
        out_specs=(vmem(), vmem(), vmem()),
        scratch_shapes=[
            pltpu.VMEM((Z, GROUP * LANE, 256), BF),
            pltpu.VMEM((Z, GROUP * LANE, 256), BF),
            pltpu.VMEM((Z, 1, GROUP * LANE), F32),
            pltpu.VMEM((Z, GROUP, HEAD_DIM, LANE), F32),
            pltpu.VMEM((4 * LANE, 256), F32),
            pltpu.VMEM((4 * LANE, 256), F32),
        ],
        compiler_params=pltpu.CompilerParams(vmem_limit_bytes=min(24 + 7 * zo, 60) << 20),
        cost_estimate=pl.CostEstimate(flops=6 * 10**10, bytes_accessed=60 << 20, transcendentals=10**7),
    )(pos, lim, q, do, o, lse, rng, kva, kvb)


def pack_kernel(wi_ref, wd_ref, wo_ref, out_ref):
    n, width = wo_ref.shape
    blocks = wi_ref.shape[1] // width
    for j in range(blocks):
        out_ref[j * n : (j + 1) * n] = wi_ref[:, j * width : (j + 1) * width]
    out_ref[blocks * n : blocks * n + wd_ref.shape[0]] = wd_ref[...]
    out_ref[blocks * n + wd_ref.shape[0] :] = wo_ref[...]


def pack_weights(wi, wd, wo):
    rows = wi.shape[0] * wi.shape[1] // wo.shape[1] + wd.shape[0] + wo.shape[0]
    return pl.pallas_call(
        pack_kernel,
        out_shape=jax.ShapeDtypeStruct((rows, wo.shape[1]), BF),
        in_specs=[vmem()] * 3,
        out_specs=vmem(),
    )(wi, wd, wo)


def hidden_grads_kernel(hb_ref, dub_ref, gb_ref, dfb_ref, out_ref, ga, gd):
    ga[...] = dot(hb_ref[...], dub_ref[...], 0, 0).astype(BF)
    gd[...] = dot(gb_ref[...], dfb_ref[...], 0, 0).astype(BF)
    n = ga.shape[0] // (2 * Z * Y)
    m = gd.shape[0] // (2 * Z * Y)
    width = gd.shape[1]
    for x in range(2):
        for z in range(Z):
            for y in range(Y):
                r = ((x * Z + z) * Y + y) * n
                for h in range(2):
                    out_ref[x * Y + y, z, h * n : (h + 1) * n] = ga[r : r + n, h * width : (h + 1) * width]
                r = ((z * Y + y) * 2 + x) * m
                out_ref[x * Y + y, z, 2 * n :] = gd[r : r + m]


def hidden_grads(hb, dub, gb, dfb):
    rows = (2 * hb.shape[1] + gb.shape[1]) // (2 * Z * Y)
    return pl.pallas_call(
        hidden_grads_kernel,
        out_shape=jax.ShapeDtypeStruct((2 * Y, Z, rows, dfb.shape[1]), BF),
        in_specs=[vmem()] * 4,
        out_specs=vmem(),
        scratch_shapes=[
            pltpu.VMEM((hb.shape[1], dub.shape[1]), BF),
            pltpu.VMEM((gb.shape[1], dfb.shape[1]), BF),
        ],
        compiler_params=pltpu.CompilerParams(vmem_limit_bytes=40 << 20),
        cost_estimate=pl.CostEstimate(flops=2 * 10**9, bytes_accessed=4 << 20, transcendentals=0),
    )(hb, dub, gb, dfb)


def normalize(values):
    centered = values - jnp.mean(values, axis=1, keepdims=True)
    inverse_root = lax.rsqrt(jnp.mean(centered * centered, axis=1, keepdims=True) + norm_epsilon)
    return (centered * inverse_root, inverse_root)


def normalize_back(grad_norm, normed, inverse_root):
    return inverse_root * (
        grad_norm
        - jnp.mean(grad_norm, axis=1, keepdims=True)
        - normed * jnp.mean(grad_norm * normed, axis=1, keepdims=True)
    )


class Place:
    def __init__(self, nb):
        self.nb = nb
        self.zo = nb // (Z * Y * C)
        self.x = lax.axis_index("head")
        b = lax.axis_index("blk")
        self.c = b % 2
        self.y = b // 2 % 2
        self.z = b // 4 % 4
        self.o = b // 16

    def move(self, a, dx=0, do=0, dz=0, dy=0, dc=0):
        pairs = []
        for x in range(2):
            for o in range(self.zo):
                for z in range(Z):
                    for y in range(Y):
                        for c in range(C):
                            src = (
                                (x + dx) % 2,
                                (o + do) % self.zo,
                                (z + dz) % Z,
                                (y + dy) % Y,
                                (c + dc) % C,
                            )
                            pairs.append((self.lin(*src), self.lin(x, o, z, y, c)))
        return lax.ppermute(a, AXES, pairs)

    def lin(self, x, o, z, y, c):
        return x * self.nb + ((o * Z + z) * Y + y) * C + c

    def swap_x_c(self, a):
        pairs = []
        for x in range(2):
            for o in range(self.zo):
                for z in range(Z):
                    for y in range(Y):
                        for c in range(C):
                            pairs.append((self.lin(c, o, z, y, x), self.lin(x, o, z, y, c)))
        return lax.ppermute(a, AXES, pairs)

    def gather_all(self, a):
        groups = [
            [self.lin(x, o, z, y, c) for x in range(2) for z in range(Z) for y in range(Y) for c in range(C)]
            for o in range(self.zo)
        ]
        got = lax.all_gather(a, AXES, axis=0, axis_index_groups=groups)
        return got.reshape((2, Z, Y, C) + a.shape)

    def reduce_chips(self, a):
        groups = [
            [self.lin(x, o, z, y, c) for x in range(2) for y in range(Y)]
            for o in range(self.zo)
            for z in range(Z)
            for c in range(C)
        ]
        return lax.psum_scatter(a, AXES, scatter_dimension=0, axis_index_groups=groups)

    def reduce_z(self, a):
        groups = [
            [self.lin(x, o, z, y, c) for z in range(Z)]
            for x in range(2)
            for o in range(self.zo)
            for y in range(Y)
            for c in range(C)
        ]
        return lax.psum_scatter(a, AXES, scatter_dimension=0, axis_index_groups=groups)

    def trade_z(self, pieces):
        return [pieces[0]] + [self.move(pieces[Z - m], dz=m) for m in range(1, Z)]

    def gather_o(self, a):
        if self.zo == 1:
            return a[None]
        got = jnp.stack([a] + [self.move(a, do=k) for k in range(1, self.zo)])
        return jnp.roll(got, self.o, axis=0)

    def scatter_o(self, a):
        if self.zo == 1:
            return a[0]
        mine = jnp.roll(a, -self.o, axis=0)
        total = mine[0].astype(F32)
        for k in range(1, self.zo):
            total = total + self.move(mine[self.zo - k], do=k).astype(F32)
        return total.astype(a.dtype)


def after(a, dep):
    first = dep[(slice(0, 1),) * dep.ndim].reshape(())
    return a + (first.astype(F32) * 0.0).astype(a.dtype)


def pick(a, index, axis):
    return lax.dynamic_index_in_dim(a, index, axis, keepdims=False)


def per_device(
    nb,
    tokens,
    doc_starts,
    w_qkv,
    b_query,
    b_value,
    w_out,
    b_out,
    gain_attn,
    shift_attn,
    w_in,
    b_in,
    w_down,
    b_down,
    gain_ffn,
    shift_ffn,
    cotangent,
):
    at = Place(nb)
    zo, x, y, z, c = at.zo, at.x, at.y, at.z, at.c
    inputs = tokens[0]
    rows, D = inputs.shape
    FF = w_in.shape[1]
    S = D // (32)
    R = S // zo
    FS = FF // 32
    FR = FS // zo
    FC = FF // 2
    total_tokens = rows * 2 * nb

    def slab(a):
        g = at.gather_o(a)
        return g.reshape((g.shape[0] * g.shape[1],) + g.shape[2:])

    small = [b_query, b_value, b_out, gain_attn, shift_attn, b_down, gain_ffn, shift_ffn]
    vec_cols = jnp.concatenate(
        [slab(v)[:, None] for v in small] + [slab(b_in).reshape(4, S).T], axis=1
    )
    vec_cols = jnp.pad(vec_cols, ((0, 0), (0, LANE - vec_cols.shape[1])))
    wq = slab(w_qkv).reshape(S, 3, Z, GROUP, HEAD_DIM)
    order = [(1, 0), (1, 1), (1, 2), (2, 2), (2, 0), (2, 1), (0, 0), (0, 1), (0, 2)]
    w4 = jnp.stack([wq[:, a, :, h] for a, h in order], axis=2)
    w4 = w4.transpose(1, 0, 2, 3).reshape(Z, S, 3 * QW)
    w4 = jnp.concatenate(
        [
            w4,
            jnp.zeros((Z, S, VEC_AT - 3 * QW), BF),
            jnp.broadcast_to(vec_cols[None], (Z, S, LANE)),
        ],
        axis=2,
    )
    w4 = jnp.roll(w4, -z, axis=0)
    got = at.trade_z([w4[m] for m in range(Z)])
    xcol = jnp.concatenate(at.trade_z([inputs] * Z), axis=0)
    wz = jnp.roll(jnp.stack(got), z, axis=0)
    wp = jnp.stack([wz, at.move(wz, dy=1), at.move(wz, dx=1), at.move(wz, dx=1, dy=1)])
    wp = after(wp, xcol[-8:])
    wc = jnp.stack([wp, at.move(wp, dc=1)]).reshape(2, 2, 2, Z, S, WPAD)
    wc = jnp.roll(wc, (c, x, y), axis=(0, 1, 2))
    wfull = wc.reshape(2, 2, 2, Z, zo, R, WPAD).transpose(1, 4, 3, 2, 0, 5, 6).reshape(D, WPAD)
    w_z = wfull[:, : 3 * QW]
    vecs = wfull[:, VEC_AT:].astype(F32).T
    bq = lax.dynamic_slice_in_dim(vecs[0], z * QW, QW, 0)
    bv = lax.dynamic_slice_in_dim(vecs[1], z * QW, QW, 0)
    bias = jnp.concatenate([jnp.zeros((QW,), F32), bv[2 * HEAD_DIM :], bv[: 2 * HEAD_DIM], bq])
    f_bout, f_g1, f_s1, f_bdown, f_g2, f_s2 = [vecs[j] for j in range(2, 8)]
    vslab = pick(wc[..., VEC_AT + 8 : VEC_AT + 12], c, 1)
    f_bin = vslab.transpose(2, 1, 0, 4, 3).reshape(Z, Y, C, zo, FR)
    f_bin = f_bin.transpose(3, 0, 1, 2, 4).reshape(FC).astype(F32)

    projected = (dot(xcol, w_z) + bias[None]).astype(BF)
    kv = projected[:, :KVW].reshape(Z, rows, KVW)
    q = projected[:, KVW:].reshape(Z, rows, QW) * jnp.asarray(HEAD_DIM**-0.5, BF)

    kvo = at.gather_o(kv)
    h1, h2 = kvo[:, : Z // 2], kvo[:, Z // 2 :]
    p1 = jnp.stack([h1, at.move(h1, dx=1)])
    p2 = jnp.stack([h2, at.move(h2, dy=1)])
    p1 = jnp.stack([p1, at.move(p1, dy=1)], axis=1)
    p2 = jnp.stack([p2, at.move(p2, dx=1)])
    kva = jnp.concatenate([p1, p2], axis=3).reshape((4,) + kvo.shape)
    kvb = at.move(kva, dc=1)

    zk = (z + jnp.arange(Z)) % Z
    first = ((((at.o * Z + zk) * Y + y) * C + c) * 2 + x) * rows
    tok = first[:, None] + jnp.arange(rows)[None]
    ends = jnp.concatenate([doc_starts[1:], jnp.full((1,), total_tokens, jnp.int32)])
    begun = tok[:, :, None] >= doc_starts[None, None, :]
    start_t = jnp.max(jnp.where(begun, doc_starts[None, None, :], 0), axis=2)
    end_t = jnp.min(jnp.where(ends[None, None, :] > tok[:, :, None], ends[None, None, :], total_tokens), axis=2)
    rng = jnp.stack([start_t, end_t], axis=1)
    lim = jnp.stack([start_t[:, 0], end_t[:, -1], start_t[:, -1], end_t[:, 0]], axis=1)
    pos = jnp.stack([x, z, y, c]).astype(jnp.int32)

    o_att, ob_att, lse = run_forward(pos, lim, q, rng, kva, kvb, zo)

    pack = pack_weights(slab(w_in), slab(w_down), slab(w_out))
    wall = at.gather_all(pack)

    def natural(a):
        a = a.reshape(2, Z, Y, C, zo, R, -1).transpose(0, 4, 1, 2, 3, 5, 6)
        return a.reshape(D, -1)

    def own_rows(first, count):
        rows_at = lax.dynamic_slice_in_dim(wall, first, count, 4)
        return natural(after(rows_at, o_att))

    win_c = [own_rows((2 * c + h) * S, S) for h in range(2)]
    wdn_c = lax.dynamic_slice(wall, (c, 0, 0, 0, 4 * S, 0), (1, Z, Y, C, FS, D))
    wdn_c = after(wdn_c, o_att).reshape(Z, Y, C, zo, FR, D)
    wdn_c = wdn_c.transpose(3, 0, 1, 2, 4, 5).reshape(FC, D)
    wo = natural(after(wall[..., 4 * S + FS :, :], o_att))

    ob = jnp.stack(at.trade_z([ob_att[k] for k in range(Z)]))
    ob = jnp.roll(ob, z, axis=0).transpose(1, 0, 2).reshape(rows, D)
    r1 = dot(ob, wo) + f_bout[None] + inputs.astype(F32)
    n1, rs1 = normalize(r1)
    h1 = n1 * f_g1[None] + f_s1[None]
    h1b = h1.astype(BF)

    def both(a):
        return jnp.roll(jnp.stack([a, at.move(a, dc=1)]), c, axis=0).reshape(2 * rows, -1)

    def split_sum(part):
        p = part.reshape(2, rows, -1)
        return pick(p, c, 0) + at.move(pick(p, 1 - c, 0), dc=1)

    hb = both(h1b)
    u = jnp.concatenate([dot(hb, w) for w in win_c], axis=1) + f_bin[None]
    g, gelu_back = jax.vjp(partial(jax.nn.gelu, approximate=True), u)
    gb = g.astype(BF)
    r2 = split_sum(dot(gb, wdn_c)) + f_bdown[None] + h1
    n2, rs2 = normalize(r2)
    layer_out = (n2 * f_g2[None] + f_s2[None]).astype(BF)
    cot = cotangent[0].astype(F32)
    g_gain2 = jnp.sum(cot * n2, axis=0)
    g_shift2 = jnp.sum(cot, axis=0)
    dr2 = normalize_back(cot * f_g2[None], n2, rs2)
    g_bdown = jnp.sum(dr2, axis=0)
    dfb = both(dr2.astype(BF))
    dub = gelu_back(dot(dfb, wdn_c, 1, 1))[0].astype(BF)
    g_bin = jnp.sum(dub.astype(F32), axis=0)
    hb_s = hb.reshape(2 * rows, 2, zo, Z, Y, C, R).transpose(0, 1, 3, 4, 5, 2, 6).reshape(2 * rows, D)
    gb_s = gb.reshape(2 * rows, zo, Z, Y, 2, FR).transpose(0, 2, 3, 4, 1, 5).reshape(2 * rows, FC)
    by_chip = hidden_grads(hb_s, dub, gb_s, dfb)
    dh1 = split_sum(dot(dub[:, :D], win_c[0], 1, 1) + dot(dub[:, D:], win_c[1], 1, 1)) + after(dr2, by_chip)
    g_gain1 = jnp.sum(dh1 * n1, axis=0)
    g_shift1 = jnp.sum(dh1, axis=0)
    dr1 = normalize_back(dh1 * f_g1[None], n1, rs1)
    g_bout = jnp.sum(dr1, axis=0)
    dab = dr1.astype(BF)
    dob = dot(dab, wo, 1, 1).astype(BF)
    dobs = jnp.roll(dob.reshape(rows, Z, QW).transpose(1, 0, 2), -z, axis=0)
    do_att = jnp.stack(at.trade_z([dobs[m] for m in range(Z)]))

    bulk = at.reduce_chips(by_chip)

    def fold(a, axis, index, **kw):
        got = at.move(pick(a, 1 - index, axis), **kw).astype(F32)
        return (pick(a, index, axis).astype(F32) + got).astype(BF)

    dq, dkva, dkvb = run_backward(pos, lim, q, do_att, o_att, lse, rng, kva, kvb, zo)
    dkvb = at.move(dkvb, dc=1)
    def add(a, b):
        return (a.astype(F32) + b.astype(F32)).astype(BF)

    n = Z // 2
    own = [(dkva[i].astype(F32) + dkvb[i].astype(F32)).astype(BF) for i in range(4)]
    g1 = at.move(jnp.stack([own[1][:, :n], own[3][:, :n]]), dy=1)
    g2 = at.move(jnp.stack([own[2][:, n:], own[3][:, n:]]), dx=1)
    k1 = add(own[0][:, :n], g1[0])
    k2 = add(own[0][:, n:], g2[0])
    g1 = at.move(add(own[2][:, :n], g1[1]), dx=1)
    g2 = at.move(add(own[1][:, n:], g2[1]), dy=1)
    dkv = jnp.concatenate([add(k1, g1), add(k2, g2)], axis=1)
    dkv = at.scatter_o(dkv).reshape(Z * rows, KVW)
    dqkv = jnp.concatenate([dkv, dq.reshape(Z * rows, QW)], axis=1)

    dxp = dot(dqkv, w_z, 1, 1).reshape(Z, rows, D).astype(BF)
    dx = sum(p.astype(F32) for p in at.trade_z([dxp[m] for m in range(Z)]))
    grad_inputs = dr1 + dx
    bulk = at.reduce_z(bulk).astype(F32)
    ga = jnp.concatenate([bulk[: 2 * S], bulk[2 * S : 4 * S]], axis=1).reshape(C, S, FC)
    g_wdn = at.swap_x_c(bulk[4 * S :].astype(BF)).astype(F32)
    g_wdn = at.scatter_o(g_wdn.reshape(zo, FR, D))
    ga_oth = at.move(pick(ga, 1 - c, 0).astype(BF), dc=1).astype(F32)
    g_win = jnp.roll(jnp.stack([pick(ga, c, 0), ga_oth]), c, axis=0)
    g_win = jnp.concatenate([g_win[0], g_win[1]], axis=1)
    g_win = at.scatter_o(g_win.reshape(zo, R, FF))

    gw = dot(xcol, dqkv, 0, 0)
    colsum = jnp.sum(dqkv.astype(F32), axis=0)
    g_bq = lax.dynamic_update_slice(jnp.zeros((D,), F32), colsum[KVW:], (z * QW,))
    sv = colsum[QW:KVW]
    sv = jnp.concatenate([sv[HEAD_DIM:], sv[:HEAD_DIM]])
    g_bv = lax.dynamic_update_slice(jnp.zeros((D,), F32), sv, (z * QW,))
    vrows = jnp.stack([g_bq, g_bv, g_bout, g_gain1, g_shift1, g_bdown, g_gain2, g_shift2])

    def by_slab(a):
        a = a.reshape(2, zo, Z, Y, C, R, -1).transpose(4, 0, 3, 2, 1, 5, 6)
        return a.reshape(C, 2, Y, Z, S, -1)

    gbin = g_bin.reshape(zo, Z, Y, C, FR).transpose(1, 2, 3, 0, 4).reshape(Z, Y, C, 4, S)
    gbin = gbin.transpose(2, 1, 0, 4, 3)
    gbin = jnp.roll(jnp.stack([gbin, jnp.zeros_like(gbin)], axis=1), c, axis=1)
    gq = jnp.concatenate(
        [
            by_slab(gw),
            jnp.zeros((C, 2, Y, Z, S, VEC_AT - 3 * QW), F32),
            by_slab(vrows.T),
            gbin,
            jnp.zeros((C, 2, Y, Z, S, LANE - 12), F32),
        ],
        axis=5,
    ).astype(BF)
    go = after(by_slab(dot(ob, dab, 0, 0)), dx).astype(BF)
    gq = jnp.concatenate([gq, go], axis=4)
    gq = fold(gq, 0, c, dc=1)
    gq = jnp.roll(gq, (-x, -y), axis=(0, 1))
    gq = (
        gq[0, 0].astype(F32)
        + at.move(gq[0, 1], dy=1).astype(F32)
        + at.move(gq[1, 0], dx=1).astype(F32)
        + at.move(gq[1, 1], dx=1, dy=1).astype(F32)
    ).astype(BF)
    gq = jnp.roll(gq, -z, axis=0)
    gq = jnp.roll(jnp.stack(at.trade_z([gq[m] for m in range(Z)])), z, axis=0).astype(F32)
    g_wout = at.scatter_o(jnp.sum(gq[:, S:], axis=0).reshape(zo, R, D))
    gq = gq[:, :S]
    gwq = gq[:, :, : 3 * QW].reshape(Z, S, 9, HEAD_DIM)
    inv = [order.index((a, h)) for a in range(3) for h in range(GROUP)]
    gwq = jnp.stack([gwq[:, :, i] for i in inv], axis=2).reshape(Z, S, 3, QW)
    gwq = gwq.transpose(1, 2, 0, 3).reshape(S, 3 * D)
    g_wqkv = at.scatter_o(gwq.reshape(zo, R, 3 * D))
    gv = jnp.sum(gq[:, :, VEC_AT:], axis=0)
    outs = [at.scatter_o(gv[:, j].reshape(zo, R)) for j in range(8)]
    g_b_in = at.scatter_o(gv[:, 8:12].T.reshape(zo, FR))
    return (
        layer_out[None],
        grad_inputs[None],
        g_wqkv,
        outs[0],
        outs[1],
        g_wout,
        outs[2],
        outs[3],
        outs[4],
        g_win,
        g_b_in,
        g_wdn,
        outs[5],
        outs[6],
        outs[7],
    )


def solution(mesh):
    nb = mesh.shape["blk"]
    w2 = P(("head", "blk"), None)
    w1 = P(("head", "blk"))
    tok = P("blk", "head", None)
    return jax.shard_map(
        partial(per_device, nb),
        mesh=mesh,
        in_specs=(tok, P(), w2, w1, w1, w2, w1, w1, w1, w2, w1, w2, w1, w1, w1, tok),
        out_specs=(tok, tok, w2, w1, w1, w2, w1, w1, w1, w2, w1, w2, w1, w1, w1),
        check_vma=False,
    )
```

```python
from functools import partial

import jax
import jax.numpy as jnp
from jax import lax
from jax.experimental import pallas as pl
from jax.experimental.pallas import tpu as pltpu
from jax.sharding import PartitionSpec as P

HEADS = 12
HEAD_DIM = 64
Z, Y, C = 4, 2, 2
GROUP = HEADS // Z
QW = GROUP * HEAD_DIM
KVW = 2 * QW
LANE = 128
WPAD = 768
VEC_AT = 640
masked_score = -1e30
norm_epsilon = 1e-06
BF = jnp.bfloat16
F32 = jnp.float32
AXES = ("head", "blk")


def dot(a, b, ca=1, cb=0):
    return lax.dot_general(a, b, (((ca,), (cb,)), ((), ())), preferred_element_type=F32)


PAIRS = ((1, 2), (0, 3))


def key_tile(pos_ref, refs, t):
    x, z, y, c = pos_ref[0], pos_ref[1], pos_ref[2], pos_ref[3]
    o, zz, yy = t // (Z * Y), lax.rem(t // Y, Z), lax.rem(t, Y)
    k, dy = lax.rem(zz - z + Z, Z), lax.rem(yy - y + Y, Y)
    places, first = [], []
    for dc in range(2):
        for dx in range(2):
            places.append((refs[dc], (dx * 2 + dy, o, k)))
            first.append(t * 4 * LANE + lax.rem(c + dc, 2) * 2 * LANE + lax.rem(x + dx, 2) * LANE)
    return places, first


def visit(pos_ref, lim_ref, t, step):
    lo, hi = t * 4 * LANE, (t + 1) * 4 * LANE
    for pair in PAIRS:
        ks = [lax.rem(zz - pos_ref[1] + Z, Z) for zz in pair]
        live = [(lim_ref[k, 1] > lo) & (lim_ref[k, 0] < hi) for k in ks]
        inside = [(lim_ref[k, 2] <= lo) & (lim_ref[k, 3] >= hi) for k in ks]
        both = live[0] & live[1]
        clear = inside[0] & inside[1]
        pl.when(both & clear)(partial(step, t, ks, False))
        pl.when(both & jnp.logical_not(clear))(partial(step, t, ks, True))
        for n in range(2):
            pl.when(live[n] & jnp.logical_not(both))(partial(step, t, ks[n : n + 1], True))


def lanes(parts):
    return parts[0] if len(parts) == 1 else jnp.concatenate(parts, axis=1)


def rows_of(parts):
    return parts[0] if len(parts) == 1 else jnp.concatenate(parts, axis=0)


def head_mask_rows(block, offset):
    lanes = lax.broadcasted_iota(jnp.int32, block.shape, 1) // HEAD_DIM
    parts = []
    for h in range(GROUP):
        parts.append(jnp.where(lanes == offset[h], block, jnp.zeros_like(block)))
    return jnp.concatenate(parts, axis=0)


def widen_q(q):
    return jnp.concatenate([q, jnp.zeros((q.shape[0], HEAD_DIM), q.dtype)], axis=1)


def widen_v(v):
    return jnp.concatenate(
        [
            jnp.zeros((v.shape[0], HEAD_DIM), v.dtype),
            v[:, 2 * HEAD_DIM :],
            v[:, : 2 * HEAD_DIM],
        ],
        axis=1,
    )


V_ROW = (2, 3, 1)


def allowed_keys(rng_ref, ks, first):
    iota = lax.broadcasted_iota(jnp.int32, (LANE, LANE), 0)
    out = []
    for k in ks:
        begin, end = rng_ref[k, 0:1, :], rng_ref[k, 1:2, :]
        ok = rows_of([(iota >= begin - f) & (iota < end - f) for f in first])
        out += [ok] * GROUP
    return lanes(out)


def attention_forward(
    zo, pos_ref, lim_ref, q_ref, rng_ref, kva_ref, kvb_ref, o_ref, ob_ref, lse_ref,
    qm, m_s, l_s, acc,
):
    for i in range(Z):
        qm[i] = head_mask_rows(widen_q(q_ref[i]), (0, 1, 2))
    m_s[...] = jnp.full(m_s.shape, masked_score, F32)
    l_s[...] = jnp.zeros(l_s.shape, F32)
    acc[...] = jnp.zeros(acc.shape, F32)

    def step(t, ks, masked):
        places, first = key_tile(pos_ref, (kva_ref, kvb_ref), t)
        kt = jnp.concatenate([ref[at] for ref, at in places], axis=0)
        s = dot(kt[:, :256], rows_of([qm[k] for k in ks]), 1, 1)
        if masked:
            ok = allowed_keys(rng_ref, ks, first)
            s = jnp.where(ok, s, masked_score)
        m_old = lanes([m_s[k] for k in ks])
        m_new = jnp.maximum(m_old, jnp.max(s, axis=0, keepdims=True))
        p = jnp.exp(s - m_new)
        if masked:
            p = jnp.where(ok, p, 0.0)
        f = jnp.exp(m_old - m_new)
        l_new = lanes([l_s[k] for k in ks]) * f + jnp.sum(p, axis=0, keepdims=True)
        pv = dot(kt[:, 128:], p.astype(BF), 0, 0)
        for n, k in enumerate(ks):
            at = n * GROUP * LANE
            m_s[k] = m_new[:, at : at + GROUP * LANE]
            l_s[k] = l_new[:, at : at + GROUP * LANE]
            for h in range(GROUP):
                r = V_ROW[h] * HEAD_DIM
                c = at + h * LANE
                acc[k, h] = acc[k, h] * f[:, c : c + LANE] + pv[r : r + HEAD_DIM, c : c + LANE]

    def body(t, carry):
        visit(pos_ref, lim_ref, t, step)
        return carry

    lax.fori_loop(0, zo * Z * Y, body, 0)
    for i in range(Z):
        l = l_s[i]
        lse_ref[i] = m_s[i] + jnp.log(l)
        parts = []
        for h in range(GROUP):
            parts.append((acc[i, h] / l[:, h * LANE : (h + 1) * LANE]).T)
        o = jnp.concatenate(parts, axis=1)
        o_ref[i] = o
        ob_ref[i] = o.astype(BF)


def attention_backward(
    zo, pos_ref, lim_ref, q_ref, do_ref, o_ref, lse_ref, rng_ref, kva_ref, kvb_ref,
    dq_ref, dkva_ref, dkvb_ref, qm, dom, delta_s, dqt, dk_s, dv_s,
):
    for i in range(Z):
        qm[i] = head_mask_rows(widen_q(q_ref[i]), (0, 1, 2))
        dom[i] = head_mask_rows(widen_v(do_ref[i]), V_ROW)
        prod = (do_ref[i].astype(F32) * o_ref[i]).T
        parts = []
        for h in range(GROUP):
            parts.append(
                jnp.sum(prod[h * HEAD_DIM : (h + 1) * HEAD_DIM], axis=0, keepdims=True)
            )
        delta_s[i] = jnp.concatenate(parts, axis=1)
    dqt[...] = jnp.zeros(dqt.shape, F32)

    def step(t, ks, masked):
        places, first = key_tile(pos_ref, (kva_ref, kvb_ref), t)
        kt = jnp.concatenate([ref[at] for ref, at in places], axis=0)
        qs = rows_of([qm[k] for k in ks])
        dos = rows_of([dom[k] for k in ks])
        s = dot(kt[:, :256], qs, 1, 1)
        p = jnp.exp(s - lanes([lse_ref[k] for k in ks]))
        if masked:
            p = jnp.where(allowed_keys(rng_ref, ks, first), p, 0.0)
        dp = dot(kt[:, 128:], dos, 1, 1)
        ds = (p * (dp - lanes([delta_s[k] for k in ks]))).astype(BF)
        dv_s[...] += dot(p.astype(BF), dos, 1, 0)
        dk_s[...] += dot(ds, qs, 1, 0)
        dq = dot(kt[:, :256], ds, 0, 0)
        for n, k in enumerate(ks):
            for h in range(GROUP):
                c = (n * GROUP + h) * LANE
                dqt[k, h] += dq[h * HEAD_DIM : (h + 1) * HEAD_DIM, c : c + LANE]

    def body(t, carry):
        dk_s[...] = jnp.zeros(dk_s.shape, F32)
        dv_s[...] = jnp.zeros(dv_s.shape, F32)
        visit(pos_ref, lim_ref, t, step)
        dk, dv = dk_s[...], dv_s[...]
        out = jnp.concatenate([dk[:, :128], dk[:, 128:] + dv[:, :128], dv[:, 128:]], axis=1)
        out = out.astype(BF)
        places, _ = key_tile(pos_ref, (dkva_ref, dkvb_ref), t)
        for n, (ref, at) in enumerate(places):
            ref[at] = out[n * LANE : (n + 1) * LANE]
        return carry

    lax.fori_loop(0, zo * Z * Y, body, 0)
    for i in range(Z):
        parts = []
        for h in range(GROUP):
            parts.append((dqt[i, h] * (HEAD_DIM**-0.5)).T)
        dq_ref[i] = jnp.concatenate(parts, axis=1).astype(BF)


def vmem():
    return pl.BlockSpec(memory_space=pltpu.VMEM)


def smem():
    return pl.BlockSpec(memory_space=pltpu.SMEM)


def run_forward(pos, lim, q, rng, kva, kvb, zo):
    return pl.pallas_call(
        partial(attention_forward, zo),
        out_shape=(
            jax.ShapeDtypeStruct((Z, LANE, QW), F32),
            jax.ShapeDtypeStruct((Z, LANE, QW), BF),
            jax.ShapeDtypeStruct((Z, 1, GROUP * LANE), F32),
        ),
        in_specs=[smem(), smem(), vmem(), vmem(), vmem(), vmem()],
        out_specs=(vmem(), vmem(), vmem()),
        scratch_shapes=[
            pltpu.VMEM((Z, GROUP * LANE, 256), BF),
            pltpu.VMEM((Z, 1, GROUP * LANE), F32),
            pltpu.VMEM((Z, 1, GROUP * LANE), F32),
            pltpu.VMEM((Z, GROUP, HEAD_DIM, LANE), F32),
        ],
        compiler_params=pltpu.CompilerParams(vmem_limit_bytes=(20 + 4 * zo) << 20),
        cost_estimate=pl.CostEstimate(flops=10**10, bytes_accessed=40 << 20, transcendentals=10**7),
    )(pos, lim, q, rng, kva, kvb)


def run_backward(pos, lim, q, do, o, lse, rng, kva, kvb, zo):
    pieces = jax.ShapeDtypeStruct((4, zo, Z, LANE, KVW), BF)
    return pl.pallas_call(
        partial(attention_backward, zo),
        out_shape=(jax.ShapeDtypeStruct((Z, LANE, QW), BF), pieces, pieces),
        in_specs=[smem(), smem()] + [vmem()] * 7,
        out_specs=(vmem(), vmem(), vmem()),
        scratch_shapes=[
            pltpu.VMEM((Z, GROUP * LANE, 256), BF),
            pltpu.VMEM((Z, GROUP * LANE, 256), BF),
            pltpu.VMEM((Z, 1, GROUP * LANE), F32),
            pltpu.VMEM((Z, GROUP, HEAD_DIM, LANE), F32),
            pltpu.VMEM((4 * LANE, 256), F32),
            pltpu.VMEM((4 * LANE, 256), F32),
        ],
        compiler_params=pltpu.CompilerParams(vmem_limit_bytes=min(24 + 7 * zo, 60) << 20),
        cost_estimate=pl.CostEstimate(flops=6 * 10**10, bytes_accessed=60 << 20, transcendentals=10**7),
    )(pos, lim, q, do, o, lse, rng, kva, kvb)


def pack_kernel(wi_ref, wd_ref, wo_ref, out_ref):
    n, width = wo_ref.shape
    blocks = wi_ref.shape[1] // width
    for j in range(blocks):
        out_ref[j * n : (j + 1) * n] = wi_ref[:, j * width : (j + 1) * width]
    out_ref[blocks * n : blocks * n + wd_ref.shape[0]] = wd_ref[...]
    out_ref[blocks * n + wd_ref.shape[0] :] = wo_ref[...]


def pack_weights(wi, wd, wo):
    rows = wi.shape[0] * wi.shape[1] // wo.shape[1] + wd.shape[0] + wo.shape[0]
    return pl.pallas_call(
        pack_kernel,
        out_shape=jax.ShapeDtypeStruct((rows, wo.shape[1]), BF),
        in_specs=[vmem()] * 3,
        out_specs=vmem(),
    )(wi, wd, wo)


def hidden_grads_kernel(hb_ref, dub_ref, gb_ref, dfb_ref, out_ref, ga, gd):
    ga[...] = dot(hb_ref[...], dub_ref[...], 0, 0).astype(BF)
    gd[...] = dot(gb_ref[...], dfb_ref[...], 0, 0).astype(BF)
    n = ga.shape[0] // (2 * Z * Y)
    m = gd.shape[0] // (2 * Z * Y)
    width = gd.shape[1]
    for x in range(2):
        for z in range(Z):
            for y in range(Y):
                r = ((x * Z + z) * Y + y) * n
                for h in range(2):
                    out_ref[x * Y + y, z, h * n : (h + 1) * n] = ga[r : r + n, h * width : (h + 1) * width]
                r = ((z * Y + y) * 2 + x) * m
                out_ref[x * Y + y, z, 2 * n :] = gd[r : r + m]


def hidden_grads(hb, dub, gb, dfb):
    rows = (2 * hb.shape[1] + gb.shape[1]) // (2 * Z * Y)
    return pl.pallas_call(
        hidden_grads_kernel,
        out_shape=jax.ShapeDtypeStruct((2 * Y, Z, rows, dfb.shape[1]), BF),
        in_specs=[vmem()] * 4,
        out_specs=vmem(),
        scratch_shapes=[
            pltpu.VMEM((hb.shape[1], dub.shape[1]), BF),
            pltpu.VMEM((gb.shape[1], dfb.shape[1]), BF),
        ],
        compiler_params=pltpu.CompilerParams(vmem_limit_bytes=40 << 20),
        cost_estimate=pl.CostEstimate(flops=2 * 10**9, bytes_accessed=4 << 20, transcendentals=0),
    )(hb, dub, gb, dfb)


def normalize(values):
    centered = values - jnp.mean(values, axis=1, keepdims=True)
    inverse_root = lax.rsqrt(jnp.mean(centered * centered, axis=1, keepdims=True) + norm_epsilon)
    return (centered * inverse_root, inverse_root)


def normalize_back(grad_norm, normed, inverse_root):
    return inverse_root * (
        grad_norm
        - jnp.mean(grad_norm, axis=1, keepdims=True)
        - normed * jnp.mean(grad_norm * normed, axis=1, keepdims=True)
    )


class Place:
    def __init__(self, nb):
        self.nb = nb
        self.zo = nb // (Z * Y * C)
        self.x = lax.axis_index("head")
        b = lax.axis_index("blk")
        self.c = b % 2
        self.y = b // 2 % 2
        self.z = b // 4 % 4
        self.o = b // 16

    def move(self, a, dx=0, do=0, dz=0, dy=0, dc=0):
        pairs = []
        for x in range(2):
            for o in range(self.zo):
                for z in range(Z):
                    for y in range(Y):
                        for c in range(C):
                            src = (
                                (x + dx) % 2,
                                (o + do) % self.zo,
                                (z + dz) % Z,
                                (y + dy) % Y,
                                (c + dc) % C,
                            )
                            pairs.append((self.lin(*src), self.lin(x, o, z, y, c)))
        return lax.ppermute(a, AXES, pairs)

    def lin(self, x, o, z, y, c):
        return x * self.nb + ((o * Z + z) * Y + y) * C + c

    def swap_x_c(self, a):
        pairs = []
        for x in range(2):
            for o in range(self.zo):
                for z in range(Z):
                    for y in range(Y):
                        for c in range(C):
                            pairs.append((self.lin(c, o, z, y, x), self.lin(x, o, z, y, c)))
        return lax.ppermute(a, AXES, pairs)

    def gather_all(self, a):
        groups = [
            [self.lin(x, o, z, y, c) for x in range(2) for z in range(Z) for y in range(Y) for c in range(C)]
            for o in range(self.zo)
        ]
        got = lax.all_gather(a, AXES, axis=0, axis_index_groups=groups)
        return got.reshape((2, Z, Y, C) + a.shape)

    def reduce_chips(self, a):
        groups = [
            [self.lin(x, o, z, y, c) for x in range(2) for y in range(Y)]
            for o in range(self.zo)
            for z in range(Z)
            for c in range(C)
        ]
        return lax.psum_scatter(a, AXES, scatter_dimension=0, axis_index_groups=groups)

    def reduce_z(self, a):
        groups = [
            [self.lin(x, o, z, y, c) for z in range(Z)]
            for x in range(2)
            for o in range(self.zo)
            for y in range(Y)
            for c in range(C)
        ]
        return lax.psum_scatter(a, AXES, scatter_dimension=0, axis_index_groups=groups)

    def trade_z(self, pieces):
        return [pieces[0]] + [self.move(pieces[Z - m], dz=m) for m in range(1, Z)]

    def gather_o(self, a):
        if self.zo == 1:
            return a[None]
        got = jnp.stack([a] + [self.move(a, do=k) for k in range(1, self.zo)])
        return jnp.roll(got, self.o, axis=0)

    def scatter_o(self, a):
        if self.zo == 1:
            return a[0]
        mine = jnp.roll(a, -self.o, axis=0)
        total = mine[0].astype(F32)
        for k in range(1, self.zo):
            total = total + self.move(mine[self.zo - k], do=k).astype(F32)
        return total.astype(a.dtype)


def after(a, dep):
    first = dep[(slice(0, 1),) * dep.ndim].reshape(())
    return a + (first.astype(F32) * 0.0).astype(a.dtype)


def pick(a, index, axis):
    return lax.dynamic_index_in_dim(a, index, axis, keepdims=False)


def per_device(
    nb,
    tokens,
    doc_starts,
    w_qkv,
    b_query,
    b_value,
    w_out,
    b_out,
    gain_attn,
    shift_attn,
    w_in,
    b_in,
    w_down,
    b_down,
    gain_ffn,
    shift_ffn,
    cotangent,
):
    at = Place(nb)
    zo, x, y, z, c = at.zo, at.x, at.y, at.z, at.c
    inputs = tokens[0]
    rows, D = inputs.shape
    FF = w_in.shape[1]
    S = D // (32)
    R = S // zo
    FS = FF // 32
    FR = FS // zo
    FC = FF // 2
    total_tokens = rows * 2 * nb

    def slab(a):
        g = at.gather_o(a)
        return g.reshape((g.shape[0] * g.shape[1],) + g.shape[2:])

    small = [b_query, b_value, b_out, gain_attn, shift_attn, b_down, gain_ffn, shift_ffn]
    vec_cols = jnp.concatenate(
        [slab(v)[:, None] for v in small] + [slab(b_in).reshape(4, S).T], axis=1
    )
    vec_cols = jnp.pad(vec_cols, ((0, 0), (0, LANE - vec_cols.shape[1])))
    wq = slab(w_qkv).reshape(S, 3, Z, GROUP, HEAD_DIM)
    order = [(1, 0), (1, 1), (1, 2), (2, 2), (2, 0), (2, 1), (0, 0), (0, 1), (0, 2)]
    w4 = jnp.stack([wq[:, a, :, h] for a, h in order], axis=2)
    w4 = w4.transpose(1, 0, 2, 3).reshape(Z, S, 3 * QW)
    w4 = jnp.concatenate(
        [
            w4,
            jnp.zeros((Z, S, VEC_AT - 3 * QW), BF),
            jnp.broadcast_to(vec_cols[None], (Z, S, LANE)),
        ],
        axis=2,
    )
    w4 = jnp.roll(w4, -z, axis=0)
    got = at.trade_z([w4[m] for m in range(Z)])
    xcol = jnp.concatenate(at.trade_z([inputs] * Z), axis=0)
    wz = jnp.roll(jnp.stack(got), z, axis=0)
    wp = jnp.stack([wz, at.move(wz, dy=1), at.move(wz, dx=1), at.move(wz, dx=1, dy=1)])
    wp = after(wp, xcol[-8:])
    wc = jnp.stack([wp, at.move(wp, dc=1)]).reshape(2, 2, 2, Z, S, WPAD)
    wc = jnp.roll(wc, (c, x, y), axis=(0, 1, 2))
    wfull = wc.reshape(2, 2, 2, Z, zo, R, WPAD).transpose(1, 4, 3, 2, 0, 5, 6).reshape(D, WPAD)
    w_z = wfull[:, : 3 * QW]
    vecs = wfull[:, VEC_AT:].astype(F32).T
    bq = lax.dynamic_slice_in_dim(vecs[0], z * QW, QW, 0)
    bv = lax.dynamic_slice_in_dim(vecs[1], z * QW, QW, 0)
    bias = jnp.concatenate([jnp.zeros((QW,), F32), bv[2 * HEAD_DIM :], bv[: 2 * HEAD_DIM], bq])
    f_bout, f_g1, f_s1, f_bdown, f_g2, f_s2 = [vecs[j] for j in range(2, 8)]
    vslab = pick(wc[..., VEC_AT + 8 : VEC_AT + 12], c, 1)
    f_bin = vslab.transpose(2, 1, 0, 4, 3).reshape(Z, Y, C, zo, FR)
    f_bin = f_bin.transpose(3, 0, 1, 2, 4).reshape(FC).astype(F32)

    projected = (dot(xcol, w_z) + bias[None]).astype(BF)
    kv = projected[:, :KVW].reshape(Z, rows, KVW)
    q = projected[:, KVW:].reshape(Z, rows, QW) * jnp.asarray(HEAD_DIM**-0.5, BF)

    kvo = at.gather_o(kv)
    h1, h2 = kvo[:, : Z // 2], kvo[:, Z // 2 :]
    p1 = jnp.stack([h1, at.move(h1, dx=1)])
    p2 = jnp.stack([h2, at.move(h2, dy=1)])
    p1 = jnp.stack([p1, at.move(p1, dy=1)], axis=1)
    p2 = jnp.stack([p2, at.move(p2, dx=1)])
    kva = jnp.concatenate([p1, p2], axis=3).reshape((4,) + kvo.shape)
    kvb = at.move(kva, dc=1)

    zk = (z + jnp.arange(Z)) % Z
    first = ((((at.o * Z + zk) * Y + y) * C + c) * 2 + x) * rows
    tok = first[:, None] + jnp.arange(rows)[None]
    ends = jnp.concatenate([doc_starts[1:], jnp.full((1,), total_tokens, jnp.int32)])
    begun = tok[:, :, None] >= doc_starts[None, None, :]
    start_t = jnp.max(jnp.where(begun, doc_starts[None, None, :], 0), axis=2)
    end_t = jnp.min(jnp.where(ends[None, None, :] > tok[:, :, None], ends[None, None, :], total_tokens), axis=2)
    rng = jnp.stack([start_t, end_t], axis=1)
    lim = jnp.stack([start_t[:, 0], end_t[:, -1], start_t[:, -1], end_t[:, 0]], axis=1)
    pos = jnp.stack([x, z, y, c]).astype(jnp.int32)

    o_att, ob_att, lse = run_forward(pos, lim, q, rng, kva, kvb, zo)

    pack = pack_weights(slab(w_in), slab(w_down), slab(w_out))
    wall = at.gather_all(pack)

    def natural(a):
        a = a.reshape(2, Z, Y, C, zo, R, -1).transpose(0, 4, 1, 2, 3, 5, 6)
        return a.reshape(D, -1)

    def own_rows(first, count):
        rows_at = lax.dynamic_slice_in_dim(wall, first, count, 4)
        return natural(rows_at)

    win_c = [own_rows((2 * c + h) * S, S) for h in range(2)]
    wdn_c = lax.dynamic_slice(wall, (c, 0, 0, 0, 4 * S, 0), (1, Z, Y, C, FS, D))
    wdn_c = wdn_c.reshape(Z, Y, C, zo, FR, D)
    wdn_c = wdn_c.transpose(3, 0, 1, 2, 4, 5).reshape(FC, D)
    wo = natural(after(wall[..., 4 * S + FS :, :], o_att))

    ob = jnp.stack(at.trade_z([ob_att[k] for k in range(Z)]))
    ob = jnp.roll(ob, z, axis=0).transpose(1, 0, 2).reshape(rows, D)
    r1 = dot(ob, wo) + f_bout[None] + inputs.astype(F32)
    n1, rs1 = normalize(r1)
    h1 = n1 * f_g1[None] + f_s1[None]
    h1b = h1.astype(BF)

    def both(a):
        return jnp.roll(jnp.stack([a, at.move(a, dc=1)]), c, axis=0).reshape(2 * rows, -1)

    def split_sum(part):
        p = part.reshape(2, rows, -1)
        return pick(p, c, 0) + at.move(pick(p, 1 - c, 0), dc=1)

    hb = both(h1b)
    u = jnp.concatenate([dot(hb, w) for w in win_c], axis=1) + f_bin[None]
    g, gelu_back = jax.vjp(partial(jax.nn.gelu, approximate=True), u)
    gb = g.astype(BF)
    r2 = split_sum(dot(gb, wdn_c)) + f_bdown[None] + h1
    n2, rs2 = normalize(r2)
    layer_out = (n2 * f_g2[None] + f_s2[None]).astype(BF)
    cot = cotangent[0].astype(F32)
    g_gain2 = jnp.sum(cot * n2, axis=0)
    g_shift2 = jnp.sum(cot, axis=0)
    dr2 = normalize_back(cot * f_g2[None], n2, rs2)
    g_bdown = jnp.sum(dr2, axis=0)
    dfb = both(dr2.astype(BF))
    dub = gelu_back(dot(dfb, wdn_c, 1, 1))[0].astype(BF)
    g_bin = jnp.sum(dub.astype(F32), axis=0)
    hb_s = hb.reshape(2 * rows, 2, zo, Z, Y, C, R).transpose(0, 1, 3, 4, 5, 2, 6).reshape(2 * rows, D)
    gb_s = gb.reshape(2 * rows, zo, Z, Y, 2, FR).transpose(0, 2, 3, 4, 1, 5).reshape(2 * rows, FC)
    by_chip = hidden_grads(hb_s, dub, gb_s, dfb)
    dh1 = split_sum(dot(dub[:, :D], win_c[0], 1, 1) + dot(dub[:, D:], win_c[1], 1, 1)) + after(dr2, by_chip)
    g_gain1 = jnp.sum(dh1 * n1, axis=0)
    g_shift1 = jnp.sum(dh1, axis=0)
    dr1 = normalize_back(dh1 * f_g1[None], n1, rs1)
    g_bout = jnp.sum(dr1, axis=0)
    dab = dr1.astype(BF)
    dob = dot(dab, wo, 1, 1).astype(BF)
    dobs = jnp.roll(dob.reshape(rows, Z, QW).transpose(1, 0, 2), -z, axis=0)
    do_att = jnp.stack(at.trade_z([dobs[m] for m in range(Z)]))

    bulk = at.reduce_chips(by_chip)

    def fold(a, axis, index, **kw):
        got = at.move(pick(a, 1 - index, axis), **kw).astype(F32)
        return (pick(a, index, axis).astype(F32) + got).astype(BF)

    dq, dkva, dkvb = run_backward(pos, lim, q, do_att, o_att, lse, rng, kva, kvb, zo)
    dkvb = at.move(dkvb, dc=1)
    def add(a, b):
        return (a.astype(F32) + b.astype(F32)).astype(BF)

    n = Z // 2
    own = [(dkva[i].astype(F32) + dkvb[i].astype(F32)).astype(BF) for i in range(4)]
    g1 = at.move(jnp.stack([own[1][:, :n], own[3][:, :n]]), dy=1)
    g2 = at.move(jnp.stack([own[2][:, n:], own[3][:, n:]]), dx=1)
    k1 = add(own[0][:, :n], g1[0])
    k2 = add(own[0][:, n:], g2[0])
    g1 = at.move(add(own[2][:, :n], g1[1]), dx=1)
    g2 = at.move(add(own[1][:, n:], g2[1]), dy=1)
    dkv = jnp.concatenate([add(k1, g1), add(k2, g2)], axis=1)
    dkv = at.scatter_o(dkv).reshape(Z * rows, KVW)
    dqkv = jnp.concatenate([dkv, dq.reshape(Z * rows, QW)], axis=1)

    dxp = dot(dqkv, w_z, 1, 1).reshape(Z, rows, D).astype(BF)
    dx = sum(p.astype(F32) for p in at.trade_z([dxp[m] for m in range(Z)]))
    grad_inputs = dr1 + dx
    bulk = at.reduce_z(bulk).astype(F32)
    ga = jnp.concatenate([bulk[: 2 * S], bulk[2 * S : 4 * S]], axis=1).reshape(C, S, FC)
    g_wdn = at.swap_x_c(bulk[4 * S :].astype(BF)).astype(F32)
    g_wdn = at.scatter_o(g_wdn.reshape(zo, FR, D))
    ga_oth = at.move(pick(ga, 1 - c, 0).astype(BF), dc=1).astype(F32)
    g_win = jnp.roll(jnp.stack([pick(ga, c, 0), ga_oth]), c, axis=0)
    g_win = jnp.concatenate([g_win[0], g_win[1]], axis=1)
    g_win = at.scatter_o(g_win.reshape(zo, R, FF))

    gw = dot(xcol, dqkv, 0, 0)
    colsum = jnp.sum(dqkv.astype(F32), axis=0)
    g_bq = lax.dynamic_update_slice(jnp.zeros((D,), F32), colsum[KVW:], (z * QW,))
    sv = colsum[QW:KVW]
    sv = jnp.concatenate([sv[HEAD_DIM:], sv[:HEAD_DIM]])
    g_bv = lax.dynamic_update_slice(jnp.zeros((D,), F32), sv, (z * QW,))
    vrows = jnp.stack([g_bq, g_bv, g_bout, g_gain1, g_shift1, g_bdown, g_gain2, g_shift2])

    def by_slab(a):
        a = a.reshape(2, zo, Z, Y, C, R, -1).transpose(4, 0, 3, 2, 1, 5, 6)
        return a.reshape(C, 2, Y, Z, S, -1)

    gbin = g_bin.reshape(zo, Z, Y, C, FR).transpose(1, 2, 3, 0, 4).reshape(Z, Y, C, 4, S)
    gbin = gbin.transpose(2, 1, 0, 4, 3)
    gbin = jnp.roll(jnp.stack([gbin, jnp.zeros_like(gbin)], axis=1), c, axis=1)
    gq = jnp.concatenate(
        [
            by_slab(gw),
            jnp.zeros((C, 2, Y, Z, S, VEC_AT - 3 * QW), F32),
            by_slab(vrows.T),
            gbin,
            jnp.zeros((C, 2, Y, Z, S, LANE - 12), F32),
        ],
        axis=5,
    ).astype(BF)
    go = after(by_slab(dot(ob, dab, 0, 0)), dx).astype(BF)
    gq = jnp.concatenate([gq, go], axis=4)
    gq = fold(gq, 0, c, dc=1)
    gq = jnp.roll(gq, (-x, -y), axis=(0, 1))
    gq = (
        gq[0, 0].astype(F32)
        + at.move(gq[0, 1], dy=1).astype(F32)
        + at.move(gq[1, 0], dx=1).astype(F32)
        + at.move(gq[1, 1], dx=1, dy=1).astype(F32)
    ).astype(BF)
    gq = jnp.roll(gq, -z, axis=0)
    gq = jnp.roll(jnp.stack(at.trade_z([gq[m] for m in range(Z)])), z, axis=0).astype(F32)
    g_wout = at.scatter_o(jnp.sum(gq[:, S:], axis=0).reshape(zo, R, D))
    gq = gq[:, :S]
    gwq = gq[:, :, : 3 * QW].reshape(Z, S, 9, HEAD_DIM)
    inv = [order.index((a, h)) for a in range(3) for h in range(GROUP)]
    gwq = jnp.stack([gwq[:, :, i] for i in inv], axis=2).reshape(Z, S, 3, QW)
    gwq = gwq.transpose(1, 2, 0, 3).reshape(S, 3 * D)
    g_wqkv = at.scatter_o(gwq.reshape(zo, R, 3 * D))
    gv = jnp.sum(gq[:, :, VEC_AT:], axis=0)
    outs = [at.scatter_o(gv[:, j].reshape(zo, R)) for j in range(8)]
    g_b_in = at.scatter_o(gv[:, 8:12].T.reshape(zo, FR))
    return (
        layer_out[None],
        grad_inputs[None],
        g_wqkv,
        outs[0],
        outs[1],
        g_wout,
        outs[2],
        outs[3],
        outs[4],
        g_win,
        g_b_in,
        g_wdn,
        outs[5],
        outs[6],
        outs[7],
    )


def solution(mesh):
    nb = mesh.shape["blk"]
    w2 = P(("head", "blk"), None)
    w1 = P(("head", "blk"))
    tok = P("blk", "head", None)
    return jax.shard_map(
        partial(per_device, nb),
        mesh=mesh,
        in_specs=(tok, P(), w2, w1, w1, w2, w1, w1, w1, w2, w1, w2, w1, w1, w1, tok),
        out_specs=(tok, tok, w2, w1, w1, w2, w1, w1, w1, w2, w1, w2, w1, w1, w1),
        check_vma=False,
    )
```
